512 devices in a mesh: region: 32 (over z_hi, y, x), sub: 16 (over z_lo, core).
Axes of the slice: x: 4, y: 4, z: 16 (z_hi: 2, z_lo: 8; z = z_hi * 8 + z_lo), core: 2. Of those that a mesh axis runs over, the one named last changes fastest.
Arguments:
- state: float32 [16384, 4, 512], P(('region', 'sub')), may hold values from -6 to 6
- register: float32 [16384, 4, 512], P(('region', 'sub')), may hold values from -6 to 6
- orders: int32 [16384], P(('region', 'sub')), may hold values from 3 to 7
- link_source: int32 [16384, 6], P(('region', 'sub')), may hold values from 0 to 5, as said below
- link_index: int32 [16384, 6], P(('region', 'sub')), may hold values from 0 to 31, as said below
- walls: int32 [16384, 6], P(('region', 'sub')), may hold values 0 or 1
- send_region: int32 [512, 2, 8], P(('region', 'sub')), may hold values from 0 to 31, as said below
- send_sub: int32 [512, 2, 8], P(('region', 'sub')), may hold values from 0 to 31, as said below
Outputs:
- new_state: float32 [16384, 4, 512], P(('region', 'sub'))
- new_register: float32 [16384, 4, 512], P(('region', 'sub'))
The draws below stay inside these ranges and needn't reach their ends.
Inputs may be any that keep to these rules, and one draw needn't show every extreme that they name: `link_source`: 0: the neighbour across this face is on the same device; 1 or 2: on the device one below or above along region (global device index minus or plus 16); 3 or 4: one below or above along sub (index minus or plus 1); 5: the face lies on the hall's outer boundary. Codes 1 to 4 occur only on faces 0 to 3 in that order, and every neighbour named exists. Device index is region index times 16 plus sub index. `link_index`: for code 0 the neighbour's element index on this device (its matching face is the opposite one); for 1 or 2 the position in that neighbour's send_region row 1 or 0, for 3 or 4 in its send_sub row 1 or 0; 0 for code 5. Neighbouring faces coincide point for point. `send_region`: element indices on the sending device; each row lists every element with a face on that side once. `send_sub`: element indices on the sending device; each row lists every element with a face on that side once.
All inputs are finite; a program needn't handle non-finite values. No bound on the sum of `walls` on one device may be relied on, other than what follows from the above.
Results may differ from the reference program's by a relative error of at most 0.0001.
Values sent between devices are 32-bit elements; how exact they have to be, the bound alone decides.
No kernel may reach another device: no remote copies, remote signals or barrier semaphores. Data moves between devices by JAX's collectives and lax.ppermute only.
A program may use at most 64 MiB of HBM per device.

```python
import math
import jax
import jax.numpy as jnp
import numpy as np
from jax import lax

BX = 4
BY = 4
BZ = 2
E_DEV = 32
E_TOTAL = 16384
CAP_R = 8
CAP_S = 8
N_REGION = 32
N_SUB = 16
DEVICES = 512


def element_layout(key):
    device_keys = jax.random.split(key, DEVICES)
    position = jax.vmap(lambda single: jax.random.permutation(single, E_DEV))(device_keys).astype(jnp.int32)
    device_rows = jnp.arange(DEVICES, dtype=jnp.int32)[:, None]
    slot_of = jnp.zeros((DEVICES, E_DEV), jnp.int32).at[device_rows, position].set(jnp.arange(E_DEV, dtype=jnp.int32)[None, :])
    return (position, slot_of)


def neighbour_tables(key):
    position, slot_of = element_layout(key)
    device = jnp.arange(DEVICES, dtype=jnp.int32)[:, None]
    region = device // N_SUB
    column = device % N_SUB
    along_x = position // (BY * BZ)
    along_y = position // BZ % BY
    along_z = position % BZ

    def local_slot(coord_x, coord_y, coord_z):
        flat_place = jnp.clip((coord_x * BY + coord_y) * BZ + coord_z, 0, E_DEV - 1)
        return jnp.take_along_axis(slot_of, flat_place, axis=1)
    sources = []
    indices = []
    inside = along_x >= 1
    sources.append(jnp.where(inside, 0, jnp.where(region >= 1, 1, 5)))
    indices.append(jnp.where(inside, local_slot(along_x - 1, along_y, along_z), jnp.where(region >= 1, along_y * BZ + along_z, 0)))
    inside = along_x <= BX - 2
    sources.append(jnp.where(inside, 0, jnp.where(region <= N_REGION - 2, 2, 5)))
    indices.append(jnp.where(inside, local_slot(along_x + 1, along_y, along_z), jnp.where(region <= N_REGION - 2, along_y * BZ + along_z, 0)))
    inside = along_y >= 1
    sources.append(jnp.where(inside, 0, jnp.where(column >= 1, 3, 5)))
    indices.append(jnp.where(inside, local_slot(along_x, along_y - 1, along_z), jnp.where(column >= 1, along_x * BZ + along_z, 0)))
    inside = along_y <= BY - 2
    sources.append(jnp.where(inside, 0, jnp.where(column <= N_SUB - 2, 4, 5)))
    indices.append(jnp.where(inside, local_slot(along_x, along_y + 1, along_z), jnp.where(column <= N_SUB - 2, along_x * BZ + along_z, 0)))
    inside = along_z >= 1
    sources.append(jnp.where(inside, 0, 5))
    indices.append(jnp.where(inside, local_slot(along_x, along_y, along_z - 1), 0))
    inside = along_z <= BZ - 2
    sources.append(jnp.where(inside, 0, 5))
    indices.append(jnp.where(inside, local_slot(along_x, along_y, along_z + 1), 0))
    source_table = jnp.stack(sources, axis=-1).reshape(DEVICES * E_DEV, 6).astype(jnp.int32)
    index_table = jnp.stack(indices, axis=-1).reshape(DEVICES * E_DEV, 6).astype(jnp.int32)
    return (source_table, index_table)


def send_lists(key):
    position, slot_of = element_layout(key)
    plane_y = jnp.arange(BY, dtype=jnp.int32)[:, None]
    plane_x = jnp.arange(BX, dtype=jnp.int32)[:, None]
    plane_z = jnp.arange(BZ, dtype=jnp.int32)[None, :]
    bottom_x = (plane_y * BZ + plane_z).reshape(-1)
    summit_x = (((BX - 1) * BY + plane_y) * BZ + plane_z).reshape(-1)
    bottom_y = (plane_x * BY * BZ + plane_z).reshape(-1)
    summit_y = ((plane_x * BY + BY - 1) * BZ + plane_z).reshape(-1)
    region_lists = jnp.stack([slot_of[:, bottom_x], slot_of[:, summit_x]], axis=1).astype(jnp.int32)
    sub_lists = jnp.stack([slot_of[:, bottom_y], slot_of[:, summit_y]], axis=1).astype(jnp.int32)
    return (region_lists, sub_lists)


def draw_link_source(key, part):
    shared = neighbour_tables(key)
    return shared[0]


def draw_link_index(key, part):
    shared = neighbour_tables(key)
    return shared[1]


def draw_send_region(key, part):
    shared = send_lists(key)
    return shared[0]


def draw_send_sub(key, part):
    shared = send_lists(key)
    return shared[1]


def plant(values, stream_key, low, high):
    dims = values.shape
    index_at = [jax.random.randint(jax.random.fold_in(stream_key, axis), (), 0, dims[axis]) for axis in range(len(dims))]
    values = values.at[tuple(index_at)].set(low)
    longest = dims.index(max(dims))
    index_at[longest] = (index_at[longest] + 1) % dims[longest]
    return values.at[tuple(index_at)].set(high)


def levels(key, dims, cuts, low, top_value):
    def one(dim, parts):
        heights = jax.random.uniform(jax.random.fold_in(jax.random.fold_in(key, 6), dim), (parts,), jnp.float32, low / len(cuts), top_value / len(cuts))
        return jnp.repeat(jnp.exp(heights), dims[dim] // parts).reshape((-1,) + (1,) * (len(dims) - dim - 1))

    gain = one(*cuts[0])
    for cut in cuts[1:]:
        gain = gain * one(*cut)
    return gain


def scatter_about(stream_key, extent, deviation, limit, cuts=(), kind=jnp.bfloat16):
    drawn = jax.random.normal(stream_key, extent, jnp.float32) * deviation
    if len(cuts) > 0:
        drawn = levels(stream_key, extent, cuts, -0.22, 0.18) * drawn
    return jnp.clip(drawn, min=-limit, max=limit).astype(kind)


def setup_inputs(seed: int = 0) -> dict:
    key_of = jax.random.split(jax.random.key(seed), 9)
    return {
        "state": scatter_about(key_of[0], (E_TOTAL, 4, 512), 1.0, 6.0, ((0, 512),), jnp.float32),
        "register": scatter_about(key_of[1], (E_TOTAL, 4, 512), 1.0, 6.0, ((0, 512),), jnp.float32),
        "orders": plant(jax.random.randint(key_of[2], (E_TOTAL,), 3, 8), jax.random.fold_in(key_of[2], 1), 3, 7).astype(jnp.int32),
        "link_source": draw_link_source(jax.random.fold_in(key_of[8], 71), 0),
        "link_index": draw_link_index(jax.random.fold_in(key_of[8], 71), 0),
        "walls": plant((jax.random.randint(key_of[5], (E_TOTAL, 6), 0, 2) < 1).astype(jnp.int32), jax.random.fold_in(key_of[5], 1), 0, 1),
        "send_region": draw_send_region(jax.random.fold_in(key_of[8], 71), 0),
        "send_sub": draw_send_sub(jax.random.fold_in(key_of[8], 71), 0),
    }


SECTION_A = (-567301805773.0 / 1357537059087.0, -2404267990393.0 / 2016746695238.0)
SECTION_B = (5161836677717.0 / 13612068292357.0, 1720146321549.0 / 2090206949498.0)
TIME_STEP = 0.02
HIGHEST = lax.Precision.HIGHEST
FACE_SIGNS = (-1.0, 1.0, -1.0, 1.0, -1.0, 1.0)
GAUSS_POSITIVE = (0.1834346424956498, 0.525532409916329, 0.7966664774136267, 0.9602898564975363)
GAUSS_MASSES = (0.362683783378362, 0.3137066458778873, 0.2223810344533745, 0.1012285362903763)

def gauss_rule():
    positive = np.array(GAUSS_POSITIVE)
    masses = np.array(GAUSS_MASSES)
    points = np.concatenate([-positive[::-1], positive])
    quad_weights = np.concatenate([masses[::-1], masses])
    return (points, quad_weights)

def legendre_table(points):
    columns_list = [points * 0.0 + 1.0, points * 1.0]
    for degree in range(1, 7):
        columns_list.append(((2 * degree + 1) * points * columns_list[degree] - degree * columns_list[degree - 1]) / (degree + 1))
    return np.stack(columns_list, axis=1)

def basis_tables():
    points, quad_weights = gauss_rule()
    degrees = np.arange(8)
    scales = np.sqrt((2.0 * degrees + 1.0) / 2.0)
    values_at = legendre_table(points) * scales[None, :]
    weighted = values_at * quad_weights[:, None]
    upper_end = scales
    lower_end = scales * (-1.0) ** degrees
    slopes = np.zeros((8, 8))
    for lower_mode in range(8):
        for upper_mode in range(8):
            if lower_mode < upper_mode and (upper_mode - lower_mode) % 2 == 1:
                slopes[lower_mode, upper_mode] = math.sqrt((2 * lower_mode + 1) * (2 * upper_mode + 1))
    return tuple((jnp.asarray(matrix, jnp.float32) for matrix in (values_at, weighted, lower_end, upper_end, slopes)))

def order_mask(orders):
    mode_ids = jnp.arange(8, dtype=jnp.int32)
    kept_modes = (mode_ids[None, :] <= orders[:, None]).astype(jnp.float32)
    return (kept_modes[:, :, None, None] * kept_modes[:, None, :, None] * kept_modes[:, None, None, :])[:, None]

def face_traces(coeffs, tables):
    values_at, weighted, lower_end, upper_end, slopes = tables
    face_list = [jnp.einsum('i,aj,bk,eqijk->eqab', lower_end, values_at, values_at, coeffs, precision=HIGHEST), jnp.einsum('i,aj,bk,eqijk->eqab', upper_end, values_at, values_at, coeffs, precision=HIGHEST), jnp.einsum('j,ai,bk,eqijk->eqab', lower_end, values_at, values_at, coeffs, precision=HIGHEST), jnp.einsum('j,ai,bk,eqijk->eqab', upper_end, values_at, values_at, coeffs, precision=HIGHEST), jnp.einsum('k,ai,bj,eqijk->eqab', lower_end, values_at, values_at, coeffs, precision=HIGHEST), jnp.einsum('k,ai,bj,eqijk->eqab', upper_end, values_at, values_at, coeffs, precision=HIGHEST)]
    stacked = jnp.stack(face_list, axis=1)
    return stacked.reshape(coeffs.shape[0], 6, 4, 64)

def wave_values(traces):
    pressure = traces[:, :, 0]
    normal = jnp.stack([FACE_SIGNS[face_id] * traces[:, face_id, 1 + face_id // 2] for face_id in range(6)], axis=1)
    return (pressure - normal, pressure + normal)

def volume_rates(coeffs, jump_half, masks, tables):
    values_at, weighted, lower_end, upper_end, slopes = tables
    elements = coeffs.shape[0]

    def slope_x(field_block):
        return jnp.einsum('mi,eijk->emjk', slopes, field_block, precision=HIGHEST)

    def slope_y(field_block):
        return jnp.einsum('mj,eijk->eimk', slopes, field_block, precision=HIGHEST)

    def slope_z(field_block):
        return jnp.einsum('mk,eijk->eijm', slopes, field_block, precision=HIGHEST)
    lifted = jnp.einsum('aj,bk,efab->efjk', weighted, weighted, jump_half.reshape(elements, 6, 8, 8), precision=HIGHEST)
    lift_x_low = jnp.einsum('i,ejk->eijk', lower_end, lifted[:, 0], precision=HIGHEST)
    lift_x_high = jnp.einsum('i,ejk->eijk', upper_end, lifted[:, 1], precision=HIGHEST)
    lift_y_low = jnp.einsum('j,eik->eijk', lower_end, lifted[:, 2], precision=HIGHEST)
    lift_y_high = jnp.einsum('j,eik->eijk', upper_end, lifted[:, 3], precision=HIGHEST)
    lift_z_low = jnp.einsum('k,eij->eijk', lower_end, lifted[:, 4], precision=HIGHEST)
    lift_z_high = jnp.einsum('k,eij->eijk', upper_end, lifted[:, 5], precision=HIGHEST)
    lift_total = lift_x_low + lift_x_high + lift_y_low + lift_y_high + lift_z_low + lift_z_high
    pressure = coeffs[:, 0]
    rate_p = lift_total - (slope_x(coeffs[:, 1]) + slope_y(coeffs[:, 2]) + slope_z(coeffs[:, 3]))
    rate_x = lift_x_low - lift_x_high - slope_x(pressure)
    rate_y = lift_y_low - lift_y_high - slope_y(pressure)
    rate_z = lift_z_low - lift_z_high - slope_z(pressure)
    return jnp.stack([rate_p, rate_x, rate_y, rate_z], axis=1) * masks

def exterior(outward, link_source, link_index, walls, send_region, send_sub):
    element = jnp.arange(E_TOTAL, dtype=jnp.int32)[:, None]
    device = element // E_DEV
    opposite = jnp.array([1, 0, 3, 2, 5, 4], dtype=jnp.int32)[None, :]
    below_r = jnp.clip(device - N_SUB, 0, DEVICES - 1)
    above_r = jnp.clip(device + N_SUB, 0, DEVICES - 1)
    below_s = jnp.clip(device - 1, 0, DEVICES - 1)
    above_s = jnp.clip(device + 1, 0, DEVICES - 1)
    region_slot = jnp.clip(link_index, 0, CAP_R - 1)
    sub_slot = jnp.clip(link_index, 0, CAP_S - 1)
    own_index = device * E_DEV + jnp.clip(link_index, 0, E_DEV - 1)
    from_below_r = below_r * E_DEV + send_region[below_r, 1, region_slot]
    from_above_r = above_r * E_DEV + send_region[above_r, 0, region_slot]
    from_below_s = below_s * E_DEV + send_sub[below_s, 1, sub_slot]
    from_above_s = above_s * E_DEV + send_sub[above_s, 0, sub_slot]
    partner = jnp.where(link_source == 1, from_below_r, own_index)
    partner = jnp.where(link_source == 2, from_above_r, partner)
    partner = jnp.where(link_source == 3, from_below_s, partner)
    partner = jnp.where(link_source == 4, from_above_s, partner)
    partner = jnp.clip(partner, 0, E_TOTAL - 1)
    gathered = outward.reshape(E_TOTAL * 6, 64)[partner * 6 + opposite]
    wall_value = walls.astype(jnp.float32)[:, :, None] * outward
    return jnp.where((link_source == 5)[:, :, None], wall_value, gathered)

def reference(state, register, orders, link_source, link_index, walls, send_region, send_sub):
    tables = basis_tables()
    masks = order_mask(orders).reshape(DEVICES, E_DEV, 1, 8, 8, 8)
    coeffs = state.reshape(DEVICES, E_DEV, 4, 8, 8, 8) * masks
    stored = register.reshape(DEVICES, E_DEV, 4, 8, 8, 8) * masks

    def block_waves(coeff_block):
        return wave_values(face_traces(coeff_block, tables))

    def block_rates(members):
        return volume_rates(members[0], members[1], members[2], tables)
    for section_index in range(2):
        inward, outward = lax.map(block_waves, coeffs)
        outside = exterior(outward.reshape(E_TOTAL, 6, 64), link_source, link_index, walls, send_region, send_sub)
        jump_half = (outside - inward.reshape(E_TOTAL, 6, 64)) * 0.5
        tendency = lax.map(block_rates, (coeffs, jump_half.reshape(DEVICES, E_DEV, 6, 64), masks))
        stored = SECTION_A[section_index] * stored + TIME_STEP * tendency
        coeffs = coeffs + SECTION_B[section_index] * stored
    return (coeffs.reshape(E_TOTAL, 4, 512), stored.reshape(E_TOTAL, 4, 512))
```

```python
import functools
import math

import jax
import jax.numpy as jnp
from jax import lax
from jax.experimental import pallas as pl
from jax.experimental.pallas import tpu as pltpu
from jax.sharding import PartitionSpec as P

SECTION_A = (-567301805773.0 / 1357537059087.0, -2404267990393.0 / 2016746695238.0)
SECTION_B = (5161836677717.0 / 13612068292357.0, 1720146321549.0 / 2090206949498.0)
TIME_STEP = 0.02
CORNER = TIME_STEP * SECTION_B[0] * 0.25


def lane_gather(x, idx):
    dims = lax.GatherDimensionNumbers(
        offset_dims=(),
        collapsed_slice_dims=(1,),
        start_index_map=(1,),
        operand_batching_dims=(0,),
        start_indices_batching_dims=(0,),
    )
    return lax.gather(
        x, idx[..., None], dims, slice_sizes=(1, 1), mode=lax.GatherScatterMode.PROMISE_IN_BOUNDS
    )


def gather_rows(x, idx):
    return jnp.stack([lane_gather(x[n], idx) for n in range(x.shape[0])])


class Consts:
    def __init__(self):
        self.lane = lax.broadcasted_iota(jnp.int32, (8, 128), 1)
        self.k = lax.broadcasted_iota(jnp.int32, (8, 128), 0)
        self.t = self.lane // 32
        self.even_k = (self.k % 2) == 0
        self.sgn_k = jnp.where(self.even_k, 1.0, -1.0)
        self.ck = (2 * self.k + 1).astype(jnp.float32)
        self.cx = [(4 * self.t + 2 * il + 1).astype(jnp.float32) for il in range(2)]

    def table(self, index, values):
        out = jnp.full((8, 128), values[0], jnp.float32)
        for n in range(1, len(values)):
            out = jnp.where(index == n, values[n], out)
        return out

    def weights(self, power):
        root = [math.sqrt((2 * n + 1) / 2.0) ** power for n in range(8)]
        along_k = self.table(self.k, root)
        rows = []
        for il in range(2):
            base = along_k * self.table(self.t, root[il::2])
            rows += [base * root[j] for j in range(8)]
        return jnp.stack(rows)


def kept(cs, order):
    rows = []
    for il in range(2):
        inner = jnp.maximum(cs.k, 2 * cs.t + il)
        rows += [jnp.maximum(inner, j) <= order for j in range(8)]
    return rows


def load_field(ref, q):
    rows = [ref[pl.ds(4 * t + q, 32, stride=16), :] for t in range(4)]
    return jnp.concatenate(rows, axis=0).T.reshape(16, 8, 128)


def store_field(ref, q, value):
    turned = value.reshape(128, 128).T
    for t in range(4):
        ref[pl.ds(4 * t + q, 32, stride=16), :] = turned[32 * t : 32 * t + 32]


def lane_rows(scratch, ref, cs):
    rows, width = ref.shape
    scratch[0:rows, 0:width] = ref[...]
    return lane_gather(scratch[...], cs.lane % width)


def row(x, n):
    return jnp.broadcast_to(x[n : n + 1, :], (8, 128))


def sums_x(b, cs):
    lane = cs.lane[None]
    r1 = pltpu.roll(b, 96, 2)
    u = b + jnp.where(lane < 96, r1, 0.0)
    uc = b + r1
    s = u + jnp.where(lane < 64, pltpu.roll(u, 64, 2), 0.0)
    tot = uc + pltpu.roll(uc, 64, 2)
    nxt = jnp.where(lane < 96, pltpu.roll(s[0:8], 96, 2), 0.0)
    return (tot[0:8] - tot[8:16], tot[0:8] + tot[8:16], jnp.concatenate([s[8:16], nxt], axis=0))


def sums_y(b, cs):
    low, high, nxt = [], [], []
    for il in range(2):
        s = [b[8 * il + j] for j in range(8)]
        for j in range(5, -1, -1):
            s[j] = s[j] + s[j + 2]
        low.append(s[0] - s[1])
        high.append(s[0] + s[1])
        nxt += s[1:] + [jnp.zeros_like(s[0])]
    return (jnp.stack(low), jnp.stack(high), jnp.stack(nxt))


def sums_z(b, cs):
    k = cs.k[None]
    r1 = pltpu.roll(b, 6, 1)
    u = b + jnp.where(k < 6, r1, 0.0)
    uc = b + r1
    s = u + jnp.where(k < 4, pltpu.roll(u, 4, 1), 0.0)
    tot = uc + pltpu.roll(uc, 4, 1)
    other = pltpu.roll(tot, 1, 1)
    return (cs.sgn_k[None] * (tot - other), tot + other, jnp.where(k < 7, pltpu.roll(s, 7, 1), 0.0))


SUMS = (sums_x, sums_y, sums_z)


def spread(axis, hs, hd, cs):
    if axis == 0:
        return (jnp.concatenate([hs, hd]), jnp.concatenate([-hd, -hs]))
    if axis == 1:
        gain_p = jnp.stack([(hs, hd)[j % 2][il] for il in range(2) for j in range(8)])
        gain_u = jnp.stack([-(hd, hs)[j % 2][il] for il in range(2) for j in range(8)])
        return (gain_p, gain_u)
    even = cs.even_k[None]
    return (jnp.where(even, hs, hd), -jnp.where(even, hd, hs))


def factors(axis, cs):
    if axis == 0:
        return [cs.cx[n // 8] for n in range(16)]
    if axis == 1:
        return [float(2 * (n % 8) + 1) for n in range(16)]
    return [cs.ck] * 16


def times(rows, value):
    return jnp.stack([value[n] * rows[n] for n in range(16)])


def traces(fields, cs):
    out, inn, nexts = [], [], []
    for axis in range(3):
        low_p, high_p, next_p = SUMS[axis](fields[0], cs)
        low_u, high_u, next_u = SUMS[axis](fields[1 + axis], cs)
        out += [low_p - low_u, high_p + high_u]
        inn += [low_p + low_u, high_p - high_u]
        nexts.append((next_p, next_u))
    return (out, inn, nexts)


def outward_xy(fields, cs):
    out = []
    for axis in range(2):
        low_p, high_p, _ = SUMS[axis](fields[0], cs)
        low_u, high_u, _ = SUMS[axis](fields[1 + axis], cs)
        out += [low_p - low_u, high_p + high_u]
    return out


def outside_waves(out, source, index, walls, cs, remote=None):
    result = []
    for f in range(6):
        src = row(source, f)
        own = row(walls, f).astype(jnp.float32)[None] * out[f]
        value = gather_rows(out[f ^ 1], cs.t * 32 + row(index, f))
        value = jnp.where((src == 5)[None], own, value)
        if f < 4:
            far = 0.0 if remote is None else remote[f]
            value = jnp.where((src == f + 1)[None], far, value)
        result.append(value)
    return result


def rates(out, inn, nexts, outside, cs):
    rate = [None] * 4
    for axis in range(3):
        low = outside[2 * axis] - inn[2 * axis]
        high = outside[2 * axis + 1] - inn[2 * axis + 1]
        gain_p, gain_u = spread(axis, (low + high) * 0.25, (high - low) * 0.25, cs)
        next_p, next_u = nexts[axis]
        fac = factors(axis, cs)
        part = times(fac, gain_p - next_u)
        rate[0] = part if axis == 0 else rate[0] + part
        rate[1 + axis] = times(fac, gain_u - next_p)
    return rate


def section_step(section, fields, stored, rate, step):
    stored = [SECTION_A[section] * stored[q] + step * rate[q] for q in range(4)]
    fields = [fields[q] + SECTION_B[section] * stored[q] for q in range(4)]
    return (fields, stored)


def pick(flag, first, second):
    return jnp.where(flag, first, second)


def even_index(axis_name):
    return jnp.full((8, 128), lax.axis_index(axis_name) % 2, jnp.int32) == 0


def read_tables(cs, scratch, orders, link_source, link_index, walls):
    order = row(lane_rows(scratch.at[0], orders, cs), 0)
    source = lane_rows(scratch.at[1], link_source, cs)
    index = lane_rows(scratch.at[2], link_index, cs)
    wall = lane_rows(scratch.at[3], walls, cs)
    return (order, source, index, wall)


def first_kernel(
    state, register, orders, link_source, link_index, walls, send_region, send_sub,
    fields_out, stored_out, region_out, even_out, odd_out, scratch,
):
    cs = Consts()
    order, source, index, wall = read_tables(cs, scratch, orders, link_source, link_index, walls)
    region_list = lane_rows(scratch.at[4], send_region, cs)
    sub_list = lane_rows(scratch.at[5], send_sub, cs)
    keep = kept(cs, order)
    scale = jnp.stack([jnp.where(keep[n], w, 0.0) for n, w in enumerate(cs.weights(1))])
    step = jnp.stack([jnp.where(c, TIME_STEP, 0.0) for c in keep])
    fields = [load_field(state, q) * scale for q in range(4)]
    stored = [load_field(register, q) * scale for q in range(4)]
    out, inn, nexts = traces(fields, cs)
    outside = outside_waves(out, source, index, wall, cs)
    rate = rates(out, inn, nexts, outside, cs)
    fields, stored = section_step(0, fields, stored, rate, step)
    for q in range(4):
        fields_out[128 * q : 128 * q + 128, :] = fields[q].reshape(128, 128)
        stored_out[128 * q : 128 * q + 128, :] = stored[q].reshape(128, 128)
    later = outward_xy(fields, cs)

    places = order
    for f in range(4):
        place = jnp.where(row(source, f) == f + 1, row(index, f), -1)
        places = jnp.where(cs.k == f + 1, place, places)
    places = places.astype(jnp.float32)

    firsts = []
    for side in range(2):
        who = row(region_list, side)
        packed = jnp.zeros((8, 128), jnp.float32)
        for kind, waves in enumerate((out[side], later[side])):
            for j in range(8):
                packed = jnp.where(cs.lane // 8 == 8 * kind + j, lane_gather(waves[j], who), packed)
        region_out[16 * side : 16 * side + 8, :] = packed
        region_out[16 * side + 8 : 16 * side + 16, :] = lane_gather(places, who)
        firsts.append(packed)
    diagonal = jnp.where(cs.lane < 64, firsts[0], pltpu.roll(firsts[1], 64, 1))

    sides = []
    for side in range(2):
        who = (cs.lane // 8) % 4 * 32 + row(sub_list, side)
        packed = jnp.zeros((8, 128), jnp.float32)
        for kind, waves in enumerate((out[2 + side], later[2 + side])):
            for il in range(2):
                packed = jnp.where(cs.lane // 32 == 2 * kind + il, lane_gather(waves[il], who), packed)
        sides.append((packed, lane_gather(places, who)))
    even = even_index("sub")
    for n in range(2):
        low, high = sides[0][n], sides[1][n]
        at = 16 * n
        even_out[at : at + 8, :] = pick(even, high, low)
        odd_out[at : at + 8, :] = pick(even, low, high)
    even_out[8:16, :] = diagonal
    odd_out[8:16, :] = diagonal


def arrivals(even_ref, odd_ref, axis_name, rows):
    even = even_index(axis_name)
    below, above = [], []
    for n in range(rows):
        a, b = even_ref[8 * n : 8 * n + 8, :], odd_ref[8 * n : 8 * n + 8, :]
        below.append(pick(even, b, a))
        above.append(pick(even, a, b))
    return (below, above)


def second_kernel(region_base, sub_even, sub_odd, even_out, odd_out):
    cs = Consts()
    sub_below, sub_above = arrivals(sub_even, sub_odd, "sub", 2)
    target = (cs.lane // 8) % 8
    whole = []
    for side in range(2):
        packed = region_base[16 * side : 16 * side + 8, :]
        info = region_base[16 * side + 8 : 16 * side + 16, :].astype(jnp.int32)
        order = row(info, 0)
        added = jnp.zeros((8, 128), jnp.float32)
        for f, message in ((2, sub_below), (3, sub_above)):
            place = row(info, f + 1)
            at = jnp.maximum(place, 0)
            total = jnp.zeros((8, 128), jnp.float32)
            for i in range(8):
                got = lane_gather(message[0], 32 * (i % 2) + 8 * (i // 2) + at)
                got = jnp.where(i <= order, got, 0.0)
                total = total - got if side == 0 and i % 2 == 1 else total + got
            total = jnp.where(place >= 0, total, 0.0)
            if f == 2:
                total = jnp.where(target % 2 == 0, total, -total)
            added = added + total
        inside = jnp.maximum(target, cs.k) <= order
        inside = jnp.logical_and(inside, cs.lane >= 64)
        added = added * (CORNER * (2 * target + 1).astype(jnp.float32))
        packed = packed + jnp.where(inside, added, 0.0)
        below, above = sub_below[1], sub_above[1]
        if side == 0:
            relay = jnp.where(cs.lane < 64, below, pltpu.roll(above, 64, 1))
        else:
            relay = jnp.where(cs.lane < 64, pltpu.roll(below, 64, 1), above)
        whole.append((packed, relay))
    even = even_index("region")
    for n in range(2):
        low, high = whole[0][n], whole[1][n]
        even_out[8 * n : 8 * n + 8, :] = pick(even, high, low)
        odd_out[8 * n : 8 * n + 8, :] = pick(even, low, high)


def third_kernel(
    fields_in, stored_in, orders, link_source, link_index, walls,
    sub_even, sub_odd, region_even, region_odd,
    state_out, register_out, scratch,
):
    cs = Consts()
    order, source, index, wall = read_tables(cs, scratch, orders, link_source, link_index, walls)
    sub_side = arrivals(sub_even, sub_odd, "sub", 3)
    region_side = arrivals(region_even, region_odd, "region", 2)
    keep = kept(cs, order)
    step = jnp.stack([jnp.where(c, TIME_STEP, 0.0) for c in keep])
    fields = [fields_in[128 * q : 128 * q + 128, :].reshape(16, 8, 128) for q in range(4)]
    stored = [stored_in[128 * q : 128 * q + 128, :].reshape(16, 8, 128) for q in range(4)]

    def arrived(kind, seconds):
        waves = []
        for side in range(2):
            at = 64 * kind + row(index, side) % 8
            message = region_side[side][0]
            waves.append(jnp.stack([lane_gather(message, at + 8 * j) for j in range(8)]))
        for side in range(2):
            at = 64 * kind + 8 * cs.t + row(index, 2 + side) % 8
            message = seconds[side] if kind else sub_side[side][0]
            waves.append(jnp.stack([lane_gather(message, at + 32 * il) for il in range(2)]))
        return waves

    first = arrived(0, None)
    first = [jnp.where((row(source, f) == f + 1)[None], first[f], 0.0) for f in range(4)]
    rate_p = None
    for axis in range(2):
        low, high = first[2 * axis], first[2 * axis + 1]
        gain_p, gain_u = spread(axis, (low + high) * 0.25, (high - low) * 0.25, cs)
        fac = factors(axis, cs)
        part = times(fac, gain_p)
        rate_p = part if axis == 0 else rate_p + part
        change = step * times(fac, gain_u)
        stored[1 + axis] = stored[1 + axis] + change
        fields[1 + axis] = fields[1 + axis] + SECTION_B[0] * change
    change = step * rate_p
    stored[0] = stored[0] + change
    fields[0] = fields[0] + SECTION_B[0] * change

    target = (cs.lane // 32) % 2 + 2 * ((cs.lane // 8) % 4)
    seconds = []
    for side in range(2):
        packed, _, info = sub_side[side]
        info = info.astype(jnp.int32)
        their_order = row(info, 0)
        added = jnp.zeros((8, 128), jnp.float32)
        for f in range(2):
            place = row(info, f + 1)
            at = 64 * side + jnp.maximum(place, 0) % 8
            relay = region_side[f][1]
            total = jnp.zeros((8, 128), jnp.float32)
            for j in range(8):
                got = jnp.where(j <= their_order, lane_gather(relay, at + 8 * j), 0.0)
                total = total - got if side == 1 and j % 2 == 1 else total + got
            total = jnp.where(place >= 0, total, 0.0)
            if f == 0:
                total = jnp.where(target % 2 == 0, total, -total)
            added = added + total
        inside = jnp.maximum(target, cs.k) <= their_order
        inside = jnp.logical_and(inside, cs.lane >= 64)
        added = added * (CORNER * (2 * target + 1).astype(jnp.float32))
        seconds.append(packed + jnp.where(inside, added, 0.0))

    out, inn, nexts = traces(fields, cs)
    outside = outside_waves(out, source, index, wall, cs, arrived(1, seconds))
    rate = rates(out, inn, nexts, outside, cs)
    fields, stored = section_step(1, fields, stored, rate, step)
    back = cs.weights(-1)
    for q in range(4):
        store_field(state_out, q, fields[q] * back)
        store_field(register_out, q, stored[q] * back)


def swap(x, axis_name, parity, count):
    pairs = []
    for i in range(parity, count - 1, 2):
        pairs += [(i, i + 1), (i + 1, i)]
    return lax.ppermute(x, axis_name, pairs)


def rows_of(*counts):
    return [jax.ShapeDtypeStruct((count, 128), jnp.float32) for count in counts]


def call(kernel, outs, scratch):
    return pl.pallas_call(
        kernel,
        out_shape=rows_of(*outs),
        scratch_shapes=scratch,
        compiler_params=pltpu.CompilerParams(vmem_limit_bytes=32 * 1024 * 1024),
    )


def body(counts, state, register, orders, link_source, link_index, walls, send_region, send_sub):
    def tiles(x):
        return x.reshape(32, 4, 4, 128).transpose(0, 2, 1, 3).reshape(512, 128)

    def untiles(x):
        return x.reshape(32, 4, 4, 128).transpose(0, 2, 1, 3).reshape(32, 4, 512)

    tables = (orders.reshape(1, 32), link_source.T, link_index.T, walls.T)
    fields, stored, region_base, even, odd = call(
        first_kernel, (512, 512, 32, 24, 24), [pltpu.VMEM((6, 8, 128), jnp.int32)]
    )(tiles(state), tiles(register), *tables, send_region[0], send_sub[0])
    sub_even = swap(even, "sub", 0, counts["sub"])
    sub_odd = swap(odd, "sub", 1, counts["sub"])
    even, odd = call(second_kernel, (16, 16), [])(region_base, sub_even, sub_odd)
    region_even = swap(even, "region", 0, counts["region"])
    region_odd = swap(odd, "region", 1, counts["region"])
    state, register = call(third_kernel, (512, 512), [pltpu.VMEM((4, 8, 128), jnp.int32)])(
        fields, stored, *tables, sub_even, sub_odd, region_even, region_odd
    )
    return (untiles(state), untiles(register))


def solution(mesh):
    both = P(("region", "sub"))
    return jax.shard_map(
        functools.partial(body, dict(mesh.shape)),
        mesh=mesh,
        in_specs=(both,) * 8,
        out_specs=(both, both),
        check_vma=False,
    )
```

```python
import functools
import math

import jax
import jax.numpy as jnp
from jax import lax
from jax.experimental import pallas as pl
from jax.experimental.pallas import tpu as pltpu
from jax.sharding import PartitionSpec as P

SECTION_A = (-567301805773.0 / 1357537059087.0, -2404267990393.0 / 2016746695238.0)
SECTION_B = (5161836677717.0 / 13612068292357.0, 1720146321549.0 / 2090206949498.0)
TIME_STEP = 0.02
CORNER = TIME_STEP * SECTION_B[0] * 0.25


def lane_gather(x, idx):
    dims = lax.GatherDimensionNumbers(
        offset_dims=(),
        collapsed_slice_dims=(1,),
        start_index_map=(1,),
        operand_batching_dims=(0,),
        start_indices_batching_dims=(0,),
    )
    return lax.gather(
        x, idx[..., None], dims, slice_sizes=(1, 1), mode=lax.GatherScatterMode.PROMISE_IN_BOUNDS
    )


def gather_rows(x, idx):
    return jnp.stack([lane_gather(x[n], idx) for n in range(x.shape[0])])


class Consts:
    def __init__(self):
        self.lane = lax.broadcasted_iota(jnp.int32, (8, 128), 1)
        self.k = lax.broadcasted_iota(jnp.int32, (8, 128), 0)
        self.t = self.lane // 32
        self.even_k = (self.k % 2) == 0
        self.sgn_k = jnp.where(self.even_k, 1.0, -1.0)
        self.ck = (2 * self.k + 1).astype(jnp.float32)
        self.cx = [(4 * self.t + 2 * il + 1).astype(jnp.float32) for il in range(2)]

    def table(self, index, values):
        out = jnp.full((8, 128), values[0], jnp.float32)
        for n in range(1, len(values)):
            out = jnp.where(index == n, values[n], out)
        return out

    def weights(self, power):
        root = [math.sqrt((2 * n + 1) / 2.0) ** power for n in range(8)]
        along_k = self.table(self.k, root)
        rows = []
        for il in range(2):
            base = along_k * self.table(self.t, root[il::2])
            rows += [base * root[j] for j in range(8)]
        return jnp.stack(rows)


def kept(cs, order):
    rows = []
    for il in range(2):
        inner = jnp.maximum(cs.k, 2 * cs.t + il)
        rows += [jnp.maximum(inner, j) <= order for j in range(8)]
    return rows


def load_field(ref, q):
    rows = [ref[pl.ds(4 * t + q, 32, stride=16), :] for t in range(4)]
    return jnp.concatenate(rows, axis=0).T.reshape(16, 8, 128)


def store_field(ref, q, value):
    turned = value.reshape(128, 128).T
    for t in range(4):
        ref[pl.ds(4 * t + q, 32, stride=16), :] = turned[32 * t : 32 * t + 32]


def lane_rows(scratch, ref, cs):
    rows, width = ref.shape
    scratch[0:rows, 0:width] = ref[...]
    return lane_gather(scratch[...], cs.lane % width)


def row(x, n):
    return jnp.broadcast_to(x[n : n + 1, :], (8, 128))


def sums_x(b, cs):
    lane = cs.lane[None]
    r1 = pltpu.roll(b, 96, 2)
    u = b + jnp.where(lane < 96, r1, 0.0)
    uc = b + r1
    s = u + jnp.where(lane < 64, pltpu.roll(u, 64, 2), 0.0)
    tot = uc + pltpu.roll(uc, 64, 2)
    nxt = jnp.where(lane < 96, pltpu.roll(s[0:8], 96, 2), 0.0)
    return (tot[0:8] - tot[8:16], tot[0:8] + tot[8:16], jnp.concatenate([s[8:16], nxt], axis=0))


def sums_y(b, cs):
    low, high, nxt = [], [], []
    for il in range(2):
        s = [b[8 * il + j] for j in range(8)]
        for j in range(5, -1, -1):
            s[j] = s[j] + s[j + 2]
        low.append(s[0] - s[1])
        high.append(s[0] + s[1])
        nxt += s[1:] + [jnp.zeros_like(s[0])]
    return (jnp.stack(low), jnp.stack(high), jnp.stack(nxt))


def sums_z(b, cs):
    k = cs.k[None]
    r1 = pltpu.roll(b, 6, 1)
    u = b + jnp.where(k < 6, r1, 0.0)
    uc = b + r1
    s = u + jnp.where(k < 4, pltpu.roll(u, 4, 1), 0.0)
    tot = uc + pltpu.roll(uc, 4, 1)
    other = pltpu.roll(tot, 1, 1)
    return (cs.sgn_k[None] * (tot - other), tot + other, jnp.where(k < 7, pltpu.roll(s, 7, 1), 0.0))


SUMS = (sums_x, sums_y, sums_z)


def spread(axis, hs, hd, cs):
    if axis == 0:
        return (jnp.concatenate([hs, hd]), jnp.concatenate([-hd, -hs]))
    if axis == 1:
        gain_p = jnp.stack([(hs, hd)[j % 2][il] for il in range(2) for j in range(8)])
        gain_u = jnp.stack([-(hd, hs)[j % 2][il] for il in range(2) for j in range(8)])
        return (gain_p, gain_u)
    even = cs.even_k[None]
    return (jnp.where(even, hs, hd), -jnp.where(even, hd, hs))


def factors(axis, cs):
    if axis == 0:
        return [cs.cx[n // 8] for n in range(16)]
    if axis == 1:
        return [float(2 * (n % 8) + 1) for n in range(16)]
    return [cs.ck] * 16


def times(rows, value):
    return jnp.stack([value[n] * rows[n] for n in range(16)])


def traces(fields, cs):
    out, inn, nexts = [], [], []
    for axis in range(3):
        low_p, high_p, next_p = SUMS[axis](fields[0], cs)
        low_u, high_u, next_u = SUMS[axis](fields[1 + axis], cs)
        out += [low_p - low_u, high_p + high_u]
        inn += [low_p + low_u, high_p - high_u]
        nexts.append((next_p, next_u))
    return (out, inn, nexts)


def outward_xy(fields, cs):
    out = []
    for axis in range(2):
        low_p, high_p, _ = SUMS[axis](fields[0], cs)
        low_u, high_u, _ = SUMS[axis](fields[1 + axis], cs)
        out += [low_p - low_u, high_p + high_u]
    return out


def outside_waves(out, source, index, walls, cs, remote=None):
    result = []
    for f in range(6):
        src = row(source, f)
        own = row(walls, f).astype(jnp.float32)[None] * out[f]
        value = gather_rows(out[f ^ 1], cs.t * 32 + row(index, f))
        value = jnp.where((src == 5)[None], own, value)
        if f < 4:
            far = 0.0 if remote is None else remote[f]
            value = jnp.where((src == f + 1)[None], far, value)
        result.append(value)
    return result


def rates(out, inn, nexts, outside, cs):
    rate = [None] * 4
    for axis in range(3):
        low = outside[2 * axis] - inn[2 * axis]
        high = outside[2 * axis + 1] - inn[2 * axis + 1]
        gain_p, gain_u = spread(axis, (low + high) * 0.25, (high - low) * 0.25, cs)
        next_p, next_u = nexts[axis]
        fac = factors(axis, cs)
        part = times(fac, gain_p - next_u)
        rate[0] = part if axis == 0 else rate[0] + part
        rate[1 + axis] = times(fac, gain_u - next_p)
    return rate


def section_step(section, fields, stored, rate, step):
    stored = [SECTION_A[section] * stored[q] + step * rate[q] for q in range(4)]
    fields = [fields[q] + SECTION_B[section] * stored[q] for q in range(4)]
    return (fields, stored)


def pick(flag, first, second):
    return jnp.where(flag, first, second)


def even_index(axis_name):
    return jnp.full((8, 128), lax.axis_index(axis_name) % 2, jnp.int32) == 0


def read_tables(cs, scratch, orders, link_source, link_index, walls):
    order = row(lane_rows(scratch.at[0], orders, cs), 0)
    source = lane_rows(scratch.at[1], link_source, cs)
    index = lane_rows(scratch.at[2], link_index, cs)
    wall = lane_rows(scratch.at[3], walls, cs)
    return (order, source, index, wall)


def first_kernel(
    state_far, register_far, orders_far, source_far, index_far, walls_far, region_far, sub_far,
    fields_out, stored_out, tables_out, region_out, odd_out, even_out,
    state, register, orders, link_source, link_index, walls, send_region, send_sub, scratch, arrived,
):
    pairs = (
        (orders_far, orders), (source_far, link_source), (index_far, link_index), (walls_far, walls),
        (region_far, send_region), (sub_far, send_sub), (state_far, state), (register_far, register),
    )
    copies = [pltpu.make_async_copy(a, b, arrived.at[n]) for n, (a, b) in enumerate(pairs)]
    for copy in copies:
        copy.start()
    cs = Consts()
    for copy in copies[:6]:
        copy.wait()
    order, source, index, wall = read_tables(cs, scratch, orders, link_source, link_index, walls)
    for n, table in enumerate((order, source, index, wall)):
        tables_out[8 * n : 8 * n + 8, :] = table
    region_list = lane_rows(scratch.at[4], send_region, cs)
    sub_list = lane_rows(scratch.at[5], send_sub, cs)
    keep = kept(cs, order)
    scale = jnp.stack([jnp.where(keep[n], w, 0.0) for n, w in enumerate(cs.weights(1))])
    step = jnp.stack([jnp.where(c, TIME_STEP, 0.0) for c in keep])
    copies[6].wait()
    fields = [load_field(state, q) * scale for q in range(4)]
    out, inn, nexts = traces(fields, cs)
    outside = outside_waves(out, source, index, wall, cs)
    rate = rates(out, inn, nexts, outside, cs)
    copies[7].wait()
    stored = [load_field(register, q) * scale for q in range(4)]
    fields, stored = section_step(0, fields, stored, rate, step)
    for q in range(4):
        fields_out[128 * q : 128 * q + 128, :] = fields[q].reshape(128, 128)
        stored_out[128 * q : 128 * q + 128, :] = stored[q].reshape(128, 128)
    later = outward_xy(fields, cs)

    places = order
    for f in range(4):
        place = jnp.where(row(source, f) == f + 1, row(index, f), -1)
        places = jnp.where(cs.k == f + 1, place, places)
    places = places.astype(jnp.float32)

    firsts = []
    for side in range(2):
        who = row(region_list, side)
        packed = jnp.zeros((8, 128), jnp.float32)
        for kind, waves in enumerate((out[side], later[side])):
            for j in range(8):
                packed = jnp.where(cs.lane // 8 == 8 * kind + j, lane_gather(waves[j], who), packed)
        region_out[16 * side : 16 * side + 8, :] = packed
        region_out[16 * side + 8 : 16 * side + 16, :] = lane_gather(places, who)
        firsts.append(packed)
    diagonal = jnp.where(cs.lane < 64, firsts[0], pltpu.roll(firsts[1], 64, 1))

    sides = []
    for side in range(2):
        who = (cs.lane // 8) % 4 * 32 + row(sub_list, side)
        packed = jnp.zeros((8, 128), jnp.float32)
        for kind, waves in enumerate((out[2 + side], later[2 + side])):
            for il in range(2):
                packed = jnp.where(cs.lane // 32 == 2 * kind + il, lane_gather(waves[il], who), packed)
        sides.append((packed, lane_gather(places, who)))
    even = even_index("sub")
    for n in range(2):
        low, high = sides[0][n], sides[1][n]
        at = 16 * n
        even_out[at : at + 8, :] = pick(even, high, low)
        odd_out[at : at + 8, :] = pick(even, low, high)
    even_out[8:16, :] = diagonal
    odd_out[8:16, :] = diagonal


def arrivals(even_ref, odd_ref, axis_name, rows):
    even = even_index(axis_name)
    below, above = [], []
    for n in range(rows):
        a, b = even_ref[8 * n : 8 * n + 8, :], odd_ref[8 * n : 8 * n + 8, :]
        below.append(pick(even, b, a))
        above.append(pick(even, a, b))
    return (below, above)


def second_kernel(region_base, sub_odd, sub_even, odd_out, even_out):
    cs = Consts()
    sub_below, sub_above = arrivals(sub_even, sub_odd, "sub", 2)
    target = (cs.lane // 8) % 8
    whole = []
    for side in range(2):
        packed = region_base[16 * side : 16 * side + 8, :]
        info = region_base[16 * side + 8 : 16 * side + 16, :].astype(jnp.int32)
        order = row(info, 0)
        added = jnp.zeros((8, 128), jnp.float32)
        for f, message in ((2, sub_below), (3, sub_above)):
            place = row(info, f + 1)
            at = jnp.maximum(place, 0)
            total = jnp.zeros((8, 128), jnp.float32)
            for i in range(8):
                got = lane_gather(message[0], 32 * (i % 2) + 8 * (i // 2) + at)
                got = jnp.where(i <= order, got, 0.0)
                total = total - got if side == 0 and i % 2 == 1 else total + got
            total = jnp.where(place >= 0, total, 0.0)
            if f == 2:
                total = jnp.where(target % 2 == 0, total, -total)
            added = added + total
        inside = jnp.maximum(target, cs.k) <= order
        inside = jnp.logical_and(inside, cs.lane >= 64)
        added = added * (CORNER * (2 * target + 1).astype(jnp.float32))
        packed = packed + jnp.where(inside, added, 0.0)
        below, above = sub_below[1], sub_above[1]
        if side == 0:
            relay = jnp.where(cs.lane < 64, below, pltpu.roll(above, 64, 1))
        else:
            relay = jnp.where(cs.lane < 64, pltpu.roll(below, 64, 1), above)
        whole.append((packed, relay))
    even = even_index("region")
    for n in range(2):
        low, high = whole[0][n], whole[1][n]
        even_out[8 * n : 8 * n + 8, :] = pick(even, high, low)
        odd_out[8 * n : 8 * n + 8, :] = pick(even, low, high)


def third_kernel(
    fields_in, stored_in, tables, sub_odd, sub_even, region_odd, region_even,
    state_far, register_far, state_out, register_out, left,
):
    cs = Consts()
    order, source, index, wall = [tables[8 * n : 8 * n + 8, :] for n in range(4)]
    sub_side = arrivals(sub_even, sub_odd, "sub", 3)
    region_side = arrivals(region_even, region_odd, "region", 2)
    keep = kept(cs, order)
    step = jnp.stack([jnp.where(c, TIME_STEP, 0.0) for c in keep])
    fields = [fields_in[128 * q : 128 * q + 128, :].reshape(16, 8, 128) for q in range(4)]
    stored = [stored_in[128 * q : 128 * q + 128, :].reshape(16, 8, 128) for q in range(4)]

    def arrived(kind, seconds):
        waves = []
        for side in range(2):
            at = 64 * kind + row(index, side) % 8
            message = region_side[side][0]
            waves.append(jnp.stack([lane_gather(message, at + 8 * j) for j in range(8)]))
        for side in range(2):
            at = 64 * kind + 8 * cs.t + row(index, 2 + side) % 8
            message = seconds[side] if kind else sub_side[side][0]
            waves.append(jnp.stack([lane_gather(message, at + 32 * il) for il in range(2)]))
        return waves

    first = arrived(0, None)
    first = [jnp.where((row(source, f) == f + 1)[None], first[f], 0.0) for f in range(4)]
    rate_p = None
    for axis in range(2):
        low, high = first[2 * axis], first[2 * axis + 1]
        gain_p, gain_u = spread(axis, (low + high) * 0.25, (high - low) * 0.25, cs)
        fac = factors(axis, cs)
        part = times(fac, gain_p)
        rate_p = part if axis == 0 else rate_p + part
        change = step * times(fac, gain_u)
        stored[1 + axis] = stored[1 + axis] + change
        fields[1 + axis] = fields[1 + axis] + SECTION_B[0] * change
    change = step * rate_p
    stored[0] = stored[0] + change
    fields[0] = fields[0] + SECTION_B[0] * change

    target = (cs.lane // 32) % 2 + 2 * ((cs.lane // 8) % 4)
    seconds = []
    for side in range(2):
        packed, _, info = sub_side[side]
        info = info.astype(jnp.int32)
        their_order = row(info, 0)
        added = jnp.zeros((8, 128), jnp.float32)
        for f in range(2):
            place = row(info, f + 1)
            at = 64 * side + jnp.maximum(place, 0) % 8
            relay = region_side[f][1]
            total = jnp.zeros((8, 128), jnp.float32)
            for j in range(8):
                got = jnp.where(j <= their_order, lane_gather(relay, at + 8 * j), 0.0)
                total = total - got if side == 1 and j % 2 == 1 else total + got
            total = jnp.where(place >= 0, total, 0.0)
            if f == 0:
                total = jnp.where(target % 2 == 0, total, -total)
            added = added + total
        inside = jnp.maximum(target, cs.k) <= their_order
        inside = jnp.logical_and(inside, cs.lane >= 64)
        added = added * (CORNER * (2 * target + 1).astype(jnp.float32))
        seconds.append(packed + jnp.where(inside, added, 0.0))

    out, inn, nexts = traces(fields, cs)
    outside = outside_waves(out, source, index, wall, cs, arrived(1, seconds))
    rate = rates(out, inn, nexts, outside, cs)
    fields, stored = section_step(1, fields, stored, rate, step)
    back = cs.weights(-1)
    copies = []
    for n, (values, ref, far) in enumerate(
        ((stored, register_out, register_far), (fields, state_out, state_far))
    ):
        for q in range(4):
            store_field(ref, q, values[q] * back)
        copies.append(pltpu.make_async_copy(ref, far, left.at[n]))
        copies[n].start()
    for copy in copies:
        copy.wait()


def swap(x, axis_name, parity, count):
    pairs = []
    for i in range(parity, count - 1, 2):
        pairs += [(i, i + 1), (i + 1, i)]
    return lax.ppermute(x, axis_name, pairs)


def call(kernel, outs, scratch, ins=None, out_space=pltpu.VMEM, kinds=None):
    kinds = [jnp.float32] * len(outs) if kinds is None else kinds
    space = pl.BlockSpec(memory_space=out_space)
    specs = {} if ins is None else dict(in_specs=[pl.BlockSpec(memory_space=pltpu.HBM)] * ins)
    return pl.pallas_call(
        kernel,
        out_shape=[jax.ShapeDtypeStruct((n, 128), kind) for n, kind in zip(outs, kinds)],
        out_specs=[space] * len(outs),
        scratch_shapes=scratch,
        compiler_params=pltpu.CompilerParams(vmem_limit_bytes=32 * 1024 * 1024),
        **specs,
    )


def body(counts, state, register, orders, link_source, link_index, walls, send_region, send_sub):
    def tiles(x):
        return x.reshape(32, 4, 4, 128).transpose(0, 2, 1, 3).reshape(512, 128)

    def untiles(x):
        return x.reshape(32, 4, 4, 128).transpose(0, 2, 1, 3).reshape(32, 4, 512)

    def held(x):
        return pltpu.with_memory_space_constraint(x, pltpu.HBM)

    whole = [pltpu.VMEM((512, 128), jnp.float32)] * 2
    small = [pltpu.VMEM(shape, jnp.int32) for shape in ((1, 32), (6, 32), (6, 32), (6, 32), (2, 8), (2, 8))]
    floats, ints = jnp.float32, jnp.int32
    fields, stored, tables, region_base, odd, even = call(
        first_kernel,
        (512, 512, 32, 32, 24, 24),
        whole + small + [pltpu.VMEM((6, 8, 128), jnp.int32), pltpu.SemaphoreType.DMA((8,))],
        ins=8,
        kinds=(floats, floats, ints, floats, floats, floats),
    )(
        held(tiles(state)), held(tiles(register)), held(orders.reshape(1, 32)), held(link_source.T),
        held(link_index.T), held(walls.T), held(send_region[0]), held(send_sub[0]),
    )
    sub_odd = swap(odd, "sub", 1, counts["sub"])
    sub_even = swap(even, "sub", 0, counts["sub"])
    odd, even = call(second_kernel, (16, 16), [])(region_base, sub_odd, sub_even)
    region_odd = swap(odd, "region", 1, counts["region"])
    region_even = swap(even, "region", 0, counts["region"])
    state, register = call(
        third_kernel, (512, 512), whole + [pltpu.SemaphoreType.DMA((2,))], out_space=pltpu.HBM
    )(fields, stored, tables, sub_odd, sub_even, region_odd, region_even)
    return (untiles(state), untiles(register))


def solution(mesh):
    both = P(("region", "sub"))
    return jax.shard_map(
        functools.partial(body, dict(mesh.shape)),
        mesh=mesh,
        in_specs=(both,) * 8,
        out_specs=(both, both),
        check_vma=False,
    )
```

```python
import functools
import math

import jax
import jax.numpy as jnp
from jax import lax
from jax.experimental import pallas as pl
from jax.experimental.pallas import tpu as pltpu
from jax.sharding import PartitionSpec as P

SECTION_A = (-567301805773.0 / 1357537059087.0, -2404267990393.0 / 2016746695238.0)
SECTION_B = (5161836677717.0 / 13612068292357.0, 1720146321549.0 / 2090206949498.0)
TIME_STEP = 0.02
CORNER = TIME_STEP * SECTION_B[0] * 0.25


def lane_gather(x, idx):
    dims = lax.GatherDimensionNumbers(
        offset_dims=(),
        collapsed_slice_dims=(1,),
        start_index_map=(1,),
        operand_batching_dims=(0,),
        start_indices_batching_dims=(0,),
    )
    return lax.gather(
        x, idx[..., None], dims, slice_sizes=(1, 1), mode=lax.GatherScatterMode.PROMISE_IN_BOUNDS
    )


def gather_rows(x, idx):
    return jnp.stack([lane_gather(x[n], idx) for n in range(x.shape[0])])


class Consts:
    def __init__(self):
        self.lane = lax.broadcasted_iota(jnp.int32, (8, 128), 1)
        self.k = lax.broadcasted_iota(jnp.int32, (8, 128), 0)
        self.t = self.lane // 32
        self.even_k = (self.k % 2) == 0
        self.sgn_k = jnp.where(self.even_k, 1.0, -1.0)
        self.ck = (2 * self.k + 1).astype(jnp.float32)
        self.cx = [(4 * self.t + 2 * il + 1).astype(jnp.float32) for il in range(2)]

    def table(self, index, values):
        out = jnp.full((8, 128), values[0], jnp.float32)
        for n in range(1, len(values)):
            out = jnp.where(index == n, values[n], out)
        return out

    def weights(self, power):
        root = [math.sqrt((2 * n + 1) / 2.0) ** power for n in range(8)]
        along_k = self.table(self.k, root)
        rows = []
        for il in range(2):
            base = along_k * self.table(self.t, root[il::2])
            rows += [base * root[j] for j in range(8)]
        return jnp.stack(rows)


def kept(cs, order):
    rows = []
    for il in range(2):
        inner = jnp.maximum(cs.k, 2 * cs.t + il)
        rows += [jnp.maximum(inner, j) <= order for j in range(8)]
    return rows


def load_field(ref, q):
    rows = [ref[pl.ds(4 * t + q, 32, stride=16), :] for t in range(4)]
    return jnp.concatenate(rows, axis=0).T.reshape(16, 8, 128)


def store_field(ref, q, value):
    turned = value.reshape(128, 128).T
    for t in range(4):
        ref[pl.ds(4 * t + q, 32, stride=16), :] = turned[32 * t : 32 * t + 32]


def lane_rows(scratch, ref, cs):
    rows, width = ref.shape
    scratch[0:rows, 0:width] = ref[...]
    return lane_gather(scratch[...], cs.lane % width)


def row(x, n):
    return jnp.broadcast_to(x[n : n + 1, :], (8, 128))


def sums_x(b, cs):
    lane = cs.lane[None]
    r1 = pltpu.roll(b, 96, 2)
    u = b + jnp.where(lane < 96, r1, 0.0)
    uc = b + r1
    s = u + jnp.where(lane < 64, pltpu.roll(u, 64, 2), 0.0)
    tot = uc + pltpu.roll(uc, 64, 2)
    nxt = jnp.where(lane < 96, pltpu.roll(s[0:8], 96, 2), 0.0)
    return (tot[0:8] - tot[8:16], tot[0:8] + tot[8:16], jnp.concatenate([s[8:16], nxt], axis=0))


def sums_y(b, cs):
    low, high, nxt = [], [], []
    for il in range(2):
        s = [b[8 * il + j] for j in range(8)]
        for j in range(5, -1, -1):
            s[j] = s[j] + s[j + 2]
        low.append(s[0] - s[1])
        high.append(s[0] + s[1])
        nxt += s[1:] + [jnp.zeros_like(s[0])]
    return (jnp.stack(low), jnp.stack(high), jnp.stack(nxt))


def sums_z(b, cs):
    k = cs.k[None]
    r1 = pltpu.roll(b, 6, 1)
    u = b + jnp.where(k < 6, r1, 0.0)
    uc = b + r1
    s = u + jnp.where(k < 4, pltpu.roll(u, 4, 1), 0.0)
    tot = uc + pltpu.roll(uc, 4, 1)
    other = pltpu.roll(tot, 1, 1)
    return (cs.sgn_k[None] * (tot - other), tot + other, jnp.where(k < 7, pltpu.roll(s, 7, 1), 0.0))


SUMS = (sums_x, sums_y, sums_z)


def spread(axis, hs, hd, cs):
    if axis == 0:
        return (jnp.concatenate([hs, hd]), jnp.concatenate([-hd, -hs]))
    if axis == 1:
        gain_p = jnp.stack([(hs, hd)[j % 2][il] for il in range(2) for j in range(8)])
        gain_u = jnp.stack([-(hd, hs)[j % 2][il] for il in range(2) for j in range(8)])
        return (gain_p, gain_u)
    even = cs.even_k[None]
    return (jnp.where(even, hs, hd), -jnp.where(even, hd, hs))


def factors(axis, cs):
    if axis == 0:
        return [cs.cx[n // 8] for n in range(16)]
    if axis == 1:
        return [float(2 * (n % 8) + 1) for n in range(16)]
    return [cs.ck] * 16


def times(rows, value):
    return jnp.stack([value[n] * rows[n] for n in range(16)])


def traces(fields, cs):
    out, inn, nexts = [], [], []
    for axis in range(3):
        low_p, high_p, next_p = SUMS[axis](fields[0], cs)
        low_u, high_u, next_u = SUMS[axis](fields[1 + axis], cs)
        out += [low_p - low_u, high_p + high_u]
        inn += [low_p + low_u, high_p - high_u]
        nexts.append((next_p, next_u))
    return (out, inn, nexts)


def outward_xy(fields, cs):
    out = []
    for axis in range(2):
        low_p, high_p, _ = SUMS[axis](fields[0], cs)
        low_u, high_u, _ = SUMS[axis](fields[1 + axis], cs)
        out += [low_p - low_u, high_p + high_u]
    return out


def outside_waves(out, source, index, walls, cs, remote=None):
    result = []
    for f in range(6):
        src = row(source, f)
        own = row(walls, f).astype(jnp.float32)[None] * out[f]
        value = gather_rows(out[f ^ 1], cs.t * 32 + row(index, f))
        value = jnp.where((src == 5)[None], own, value)
        if f < 4:
            far = 0.0 if remote is None else remote[f]
            value = jnp.where((src == f + 1)[None], far, value)
        result.append(value)
    return result


def rates(out, inn, nexts, outside, cs):
    rate = [None] * 4
    for axis in range(3):
        low = outside[2 * axis] - inn[2 * axis]
        high = outside[2 * axis + 1] - inn[2 * axis + 1]
        gain_p, gain_u = spread(axis, (low + high) * 0.25, (high - low) * 0.25, cs)
        next_p, next_u = nexts[axis]
        fac = factors(axis, cs)
        part = times(fac, gain_p - next_u)
        rate[0] = part if axis == 0 else rate[0] + part
        rate[1 + axis] = times(fac, gain_u - next_p)
    return rate


def section_step(section, fields, stored, rate, step):
    stored = [SECTION_A[section] * stored[q] + step * rate[q] for q in range(4)]
    fields = [fields[q] + SECTION_B[section] * stored[q] for q in range(4)]
    return (fields, stored)


def pick(flag, first, second):
    return jnp.where(flag, first, second)


def even_index(axis_name):
    return jnp.full((8, 128), lax.axis_index(axis_name) % 2, jnp.int32) == 0


def read_tables(cs, scratch, orders, link_source, link_index, walls):
    order = row(lane_rows(scratch.at[0], orders, cs), 0)
    source = lane_rows(scratch.at[1], link_source, cs)
    index = lane_rows(scratch.at[2], link_index, cs)
    wall = lane_rows(scratch.at[3], walls, cs)
    return (order, source, index, wall)


def first_kernel(
    state_far, register_far, orders_far, source_far, index_far, walls_far, region_far, sub_far,
    fields_out, stored_out, tables_out, region_out, odd_out, even_out,
    state, register, orders, link_source, link_index, walls, send_region, send_sub, scratch, arrived,
):
    pairs = (
        (orders_far, orders), (source_far, link_source), (index_far, link_index), (walls_far, walls),
        (region_far, send_region), (sub_far, send_sub), (state_far, state), (register_far, register),
    )
    copies = [pltpu.make_async_copy(a, b, arrived.at[n]) for n, (a, b) in enumerate(pairs)]
    for copy in copies:
        copy.start()
    cs = Consts()
    for copy in copies[:6]:
        copy.wait()
    order, source, index, wall = read_tables(cs, scratch, orders, link_source, link_index, walls)
    for n, table in enumerate((order, source, index, wall)):
        tables_out[8 * n : 8 * n + 8, :] = table
    region_list = lane_rows(scratch.at[4], send_region, cs)
    sub_list = lane_rows(scratch.at[5], send_sub, cs)
    keep = kept(cs, order)
    scale = jnp.stack([jnp.where(keep[n], w, 0.0) for n, w in enumerate(cs.weights(1))])
    step = jnp.stack([jnp.where(c, TIME_STEP, 0.0) for c in keep])
    copies[6].wait()
    fields = [load_field(state, q) * scale for q in range(4)]
    out, inn, nexts = traces(fields, cs)
    outside = outside_waves(out, source, index, wall, cs)
    rate = rates(out, inn, nexts, outside, cs)
    copies[7].wait()
    stored = [load_field(register, q) * scale for q in range(4)]
    fields, stored = section_step(0, fields, stored, rate, step)
    for q in range(4):
        fields_out[128 * q : 128 * q + 128, :] = fields[q].reshape(128, 128)
        stored_out[128 * q : 128 * q + 128, :] = stored[q].reshape(128, 128)
    later = outward_xy(fields, cs)

    places = order
    for f in range(4):
        place = jnp.where(row(source, f) == f + 1, row(index, f), -1)
        places = jnp.where(cs.k == f + 1, place, places)
    places = places.astype(jnp.float32)

    firsts = []
    for side in range(2):
        who = row(region_list, side)
        packed = jnp.zeros((8, 128), jnp.float32)
        for kind, waves in enumerate((out[side], later[side])):
            for j in range(8):
                packed = jnp.where(cs.lane // 8 == 8 * kind + j, lane_gather(waves[j], who), packed)
        region_out[16 * side : 16 * side + 8, :] = packed
        region_out[16 * side + 8 : 16 * side + 16, :] = lane_gather(places, who)
        firsts.append(packed)
    diagonal = jnp.where(cs.lane < 64, firsts[0], pltpu.roll(firsts[1], 64, 1))

    sides = []
    for side in range(2):
        who = (cs.lane // 8) % 4 * 32 + row(sub_list, side)
        packed = jnp.zeros((8, 128), jnp.float32)
        for kind, waves in enumerate((out[2 + side], later[2 + side])):
            for il in range(2):
                packed = jnp.where(cs.lane // 32 == 2 * kind + il, lane_gather(waves[il], who), packed)
        sides.append((packed, lane_gather(places, who)))
    even = even_index("sub")
    for n in range(2):
        low, high = sides[0][n], sides[1][n]
        at = 16 * n
        even_out[at : at + 8, :] = pick(even, high, low)
        odd_out[at : at + 8, :] = pick(even, low, high)
    even_out[8:16, :] = diagonal
    odd_out[8:16, :] = diagonal


def arrivals(even_ref, odd_ref, axis_name, rows):
    even = even_index(axis_name)
    below, above = [], []
    for n in range(rows):
        a, b = even_ref[8 * n : 8 * n + 8, :], odd_ref[8 * n : 8 * n + 8, :]
        if even_ref.shape[0] > odd_ref.shape[0]:
            other = odd_ref.shape[0] + 8 * n
            a = pick(even, even_ref[other : other + 8, :], a)
        below.append(pick(even, b, a))
        above.append(pick(even, a, b))
    return (below, above)


def second_kernel(region_base, sub_odd, sub_even, odd_out, even_out):
    cs = Consts()
    sub_below, sub_above = arrivals(sub_even, sub_odd, "sub", 2)
    target = (cs.lane // 8) % 8
    whole = []
    for side in range(2):
        packed = region_base[16 * side : 16 * side + 8, :]
        info = region_base[16 * side + 8 : 16 * side + 16, :].astype(jnp.int32)
        order = row(info, 0)
        added = jnp.zeros((8, 128), jnp.float32)
        for f, message in ((2, sub_below), (3, sub_above)):
            place = row(info, f + 1)
            at = jnp.maximum(place, 0)
            total = jnp.zeros((8, 128), jnp.float32)
            for i in range(8):
                got = lane_gather(message[0], 32 * (i % 2) + 8 * (i // 2) + at)
                got = jnp.where(i <= order, got, 0.0)
                total = total - got if side == 0 and i % 2 == 1 else total + got
            total = jnp.where(place >= 0, total, 0.0)
            if f == 2:
                total = jnp.where(target % 2 == 0, total, -total)
            added = added + total
        inside = jnp.maximum(target, cs.k) <= order
        inside = jnp.logical_and(inside, cs.lane >= 64)
        added = added * (CORNER * (2 * target + 1).astype(jnp.float32))
        packed = packed + jnp.where(inside, added, 0.0)
        below, above = sub_below[1], sub_above[1]
        if side == 0:
            relay = jnp.where(cs.lane < 64, below, pltpu.roll(above, 64, 1))
        else:
            relay = jnp.where(cs.lane < 64, pltpu.roll(below, 64, 1), above)
        whole.append((packed, relay))
    even = even_index("region")
    for n in range(2):
        low, high = whole[0][n], whole[1][n]
        even_out[8 * n : 8 * n + 8, :] = pick(even, high, low)
        odd_out[8 * n : 8 * n + 8, :] = pick(even, low, high)


def third_kernel(
    fields_in, stored_in, tables, sub_odd, sub_even, region_odd, region_even,
    state_far, register_far, state_out, register_out, left,
):
    cs = Consts()
    order, source, index, wall = [tables[8 * n : 8 * n + 8, :] for n in range(4)]
    sub_side = arrivals(sub_even, sub_odd, "sub", 3)
    region_side = arrivals(region_even, region_odd, "region", 2)
    keep = kept(cs, order)
    step = jnp.stack([jnp.where(c, TIME_STEP, 0.0) for c in keep])
    fields = [fields_in[128 * q : 128 * q + 128, :].reshape(16, 8, 128) for q in range(4)]
    stored = [stored_in[128 * q : 128 * q + 128, :].reshape(16, 8, 128) for q in range(4)]

    def arrived(kind, seconds):
        waves = []
        for side in range(2):
            at = 64 * kind + row(index, side) % 8
            message = region_side[side][0]
            waves.append(jnp.stack([lane_gather(message, at + 8 * j) for j in range(8)]))
        for side in range(2):
            at = 64 * kind + 8 * cs.t + row(index, 2 + side) % 8
            message = seconds[side] if kind else sub_side[side][0]
            waves.append(jnp.stack([lane_gather(message, at + 32 * il) for il in range(2)]))
        return waves

    first = arrived(0, None)
    first = [jnp.where((row(source, f) == f + 1)[None], first[f], 0.0) for f in range(4)]
    rate_p = None
    for axis in range(2):
        low, high = first[2 * axis], first[2 * axis + 1]
        gain_p, gain_u = spread(axis, (low + high) * 0.25, (high - low) * 0.25, cs)
        fac = factors(axis, cs)
        part = times(fac, gain_p)
        rate_p = part if axis == 0 else rate_p + part
        change = step * times(fac, gain_u)
        stored[1 + axis] = stored[1 + axis] + change
        fields[1 + axis] = fields[1 + axis] + SECTION_B[0] * change
    change = step * rate_p
    stored[0] = stored[0] + change
    fields[0] = fields[0] + SECTION_B[0] * change

    target = (cs.lane // 32) % 2 + 2 * ((cs.lane // 8) % 4)
    seconds = []
    for side in range(2):
        packed, _, info = sub_side[side]
        info = info.astype(jnp.int32)
        their_order = row(info, 0)
        added = jnp.zeros((8, 128), jnp.float32)
        for f in range(2):
            place = row(info, f + 1)
            at = 64 * side + jnp.maximum(place, 0) % 8
            relay = region_side[f][1]
            total = jnp.zeros((8, 128), jnp.float32)
            for j in range(8):
                got = jnp.where(j <= their_order, lane_gather(relay, at + 8 * j), 0.0)
                total = total - got if side == 1 and j % 2 == 1 else total + got
            total = jnp.where(place >= 0, total, 0.0)
            if f == 0:
                total = jnp.where(target % 2 == 0, total, -total)
            added = added + total
        inside = jnp.maximum(target, cs.k) <= their_order
        inside = jnp.logical_and(inside, cs.lane >= 64)
        added = added * (CORNER * (2 * target + 1).astype(jnp.float32))
        seconds.append(packed + jnp.where(inside, added, 0.0))

    out, inn, nexts = traces(fields, cs)
    outside = outside_waves(out, source, index, wall, cs, arrived(1, seconds))
    rate = rates(out, inn, nexts, outside, cs)
    fields, stored = section_step(1, fields, stored, rate, step)
    back = cs.weights(-1)
    copies = []
    for n, (values, ref, far) in enumerate(
        ((stored, register_out, register_far), (fields, state_out, state_far))
    ):
        for q in range(4):
            store_field(ref, q, values[q] * back)
        copies.append(pltpu.make_async_copy(ref, far, left.at[n]))
        copies[n].start()
    for copy in copies:
        copy.wait()


def swap(x, axis_name, parity, count):
    pairs = []
    for i in range(parity, count - 1, 2):
        pairs += [(i, i + 1), (i + 1, i)]
    return lax.ppermute(x, axis_name, pairs)


def gather_pairs(x, axis_name, count):
    groups = [[i, i + 1] for i in range(0, count, 2)]
    return lax.all_gather(x, axis_name, axis_index_groups=groups, tiled=True)


def call(kernel, outs, scratch, ins=None, out_space=pltpu.VMEM, kinds=None):
    kinds = [jnp.float32] * len(outs) if kinds is None else kinds
    space = pl.BlockSpec(memory_space=out_space)
    specs = {} if ins is None else dict(in_specs=[pl.BlockSpec(memory_space=pltpu.HBM)] * ins)
    return pl.pallas_call(
        kernel,
        out_shape=[jax.ShapeDtypeStruct((n, 128), kind) for n, kind in zip(outs, kinds)],
        out_specs=[space] * len(outs),
        scratch_shapes=scratch,
        compiler_params=pltpu.CompilerParams(vmem_limit_bytes=32 * 1024 * 1024),
        **specs,
    )


def body(counts, state, register, orders, link_source, link_index, walls, send_region, send_sub):
    def tiles(x):
        return x.reshape(32, 4, 4, 128).transpose(0, 2, 1, 3).reshape(512, 128)

    def untiles(x):
        return x.reshape(32, 4, 4, 128).transpose(0, 2, 1, 3).reshape(32, 4, 512)

    def held(x):
        return pltpu.with_memory_space_constraint(x, pltpu.HBM)

    whole = [pltpu.VMEM((512, 128), jnp.float32)] * 2
    small = [pltpu.VMEM(shape, jnp.int32) for shape in ((1, 32), (6, 32), (6, 32), (6, 32), (2, 8), (2, 8))]
    floats, ints = jnp.float32, jnp.int32
    fields, stored, tables, region_base, odd, even = call(
        first_kernel,
        (512, 512, 32, 32, 24, 24),
        whole + small + [pltpu.VMEM((6, 8, 128), jnp.int32), pltpu.SemaphoreType.DMA((8,))],
        ins=8,
        kinds=(floats, floats, ints, floats, floats, floats),
    )(
        held(tiles(state)), held(tiles(register)), held(orders.reshape(1, 32)), held(link_source.T),
        held(link_index.T), held(walls.T), held(send_region[0]), held(send_sub[0]),
    )
    sub_odd = swap(odd, "sub", 1, counts["sub"])
    sub_even = gather_pairs(even, "sub", counts["sub"])
    odd, even = call(second_kernel, (16, 16), [])(region_base, sub_odd, sub_even)
    region_odd = swap(odd, "region", 1, counts["region"])
    region_even = gather_pairs(even, "region", counts["region"])
    state, register = call(
        third_kernel, (512, 512), whole + [pltpu.SemaphoreType.DMA((2,))], out_space=pltpu.HBM
    )(fields, stored, tables, sub_odd, sub_even, region_odd, region_even)
    return (untiles(state), untiles(register))


def solution(mesh):
    both = P(("region", "sub"))
    return jax.shard_map(
        functools.partial(body, dict(mesh.shape)),
        mesh=mesh,
        in_specs=(both,) * 8,
        out_specs=(both, both),
        check_vma=False,
    )
```

```python
import functools
import math

import jax
import jax.numpy as jnp
from jax import lax
from jax.experimental import pallas as pl
from jax.experimental.pallas import tpu as pltpu
from jax.sharding import PartitionSpec as P

SECTION_A = (-567301805773.0 / 1357537059087.0, -2404267990393.0 / 2016746695238.0)
SECTION_B = (5161836677717.0 / 13612068292357.0, 1720146321549.0 / 2090206949498.0)
TIME_STEP = 0.02
CORNER = TIME_STEP * SECTION_B[0] * 0.25


def lane_gather(x, idx):
    dims = lax.GatherDimensionNumbers(
        offset_dims=(),
        collapsed_slice_dims=(1,),
        start_index_map=(1,),
        operand_batching_dims=(0,),
        start_indices_batching_dims=(0,),
    )
    return lax.gather(
        x, idx[..., None], dims, slice_sizes=(1, 1), mode=lax.GatherScatterMode.PROMISE_IN_BOUNDS
    )


def gather_rows(x, idx):
    return jnp.stack([lane_gather(x[n], idx) for n in range(x.shape[0])])


class Consts:
    def __init__(self):
        self.lane = lax.broadcasted_iota(jnp.int32, (8, 128), 1)
        self.k = lax.broadcasted_iota(jnp.int32, (8, 128), 0)
        self.t = self.lane // 32
        self.even_k = (self.k % 2) == 0
        self.sgn_k = jnp.where(self.even_k, 1.0, -1.0)
        self.ck = (2 * self.k + 1).astype(jnp.float32)
        self.cx = [(4 * self.t + 2 * il + 1).astype(jnp.float32) for il in range(2)]

    def table(self, index, values):
        out = jnp.full((8, 128), values[0], jnp.float32)
        for n in range(1, len(values)):
            out = jnp.where(index == n, values[n], out)
        return out

    def weights(self, power):
        root = [math.sqrt((2 * n + 1) / 2.0) ** power for n in range(8)]
        along_k = self.table(self.k, root)
        rows = []
        for il in range(2):
            base = along_k * self.table(self.t, root[il::2])
            rows += [base * root[j] for j in range(8)]
        return jnp.stack(rows)


def kept(cs, order):
    rows = []
    for il in range(2):
        inner = jnp.maximum(cs.k, 2 * cs.t + il)
        rows += [jnp.maximum(inner, j) <= order for j in range(8)]
    return rows


def load_field(ref, q):
    rows = [ref[pl.ds(4 * t + q, 32, stride=16), :] for t in range(4)]
    return jnp.concatenate(rows, axis=0).T.reshape(16, 8, 128)


def store_field(ref, q, value):
    turned = value.reshape(128, 128).T
    for t in range(4):
        ref[pl.ds(4 * t + q, 32, stride=16), :] = turned[32 * t : 32 * t + 32]


def lane_rows(scratch, ref, cs):
    rows, width = ref.shape
    scratch[0:rows, 0:width] = ref[...]
    return lane_gather(scratch[...], cs.lane % width)


def row(x, n):
    return jnp.broadcast_to(x[n : n + 1, :], (8, 128))


def sums_x(b, cs):
    lane = cs.lane[None]
    r1, r2, r3 = [pltpu.roll(b, n, 2) for n in (96, 64, 32)]
    above = jnp.where(lane < 96, r1, 0.0) + (
        jnp.where(lane < 64, r2, 0.0) + jnp.where(lane < 32, r3, 0.0)
    )
    tot = (b + r1) + (r2 + r3)
    nxt = jnp.concatenate([b[8:16] + above[8:16], above[0:8]], axis=0)
    return (tot[0:8] - tot[8:16], tot[0:8] + tot[8:16], nxt)


def sums_y(b, cs):
    low, high, nxt = [], [], []
    for il in range(2):
        s = [b[8 * il + j] for j in range(8)]
        for j in range(5, -1, -1):
            s[j] = s[j] + s[j + 2]
        low.append(s[0] - s[1])
        high.append(s[0] + s[1])
        nxt += s[1:] + [jnp.zeros_like(s[0])]
    return (jnp.stack(low), jnp.stack(high), jnp.stack(nxt))


def sums_z(b, cs):
    k = cs.k[None]
    r1 = pltpu.roll(b, 6, 1)
    u = b + jnp.where(k < 6, r1, 0.0)
    uc = b + r1
    s = u + jnp.where(k < 4, pltpu.roll(u, 4, 1), 0.0)
    tot = uc + pltpu.roll(uc, 4, 1)
    other = pltpu.roll(tot, 1, 1)
    return (cs.sgn_k[None] * (tot - other), tot + other, jnp.where(k < 7, pltpu.roll(s, 7, 1), 0.0))


SUMS = (sums_x, sums_y, sums_z)


def spread(axis, hs, hd, cs):
    if axis == 0:
        return (jnp.concatenate([hs, hd]), jnp.concatenate([-hd, -hs]))
    if axis == 1:
        gain_p = jnp.stack([(hs, hd)[j % 2][il] for il in range(2) for j in range(8)])
        gain_u = jnp.stack([-(hd, hs)[j % 2][il] for il in range(2) for j in range(8)])
        return (gain_p, gain_u)
    even = cs.even_k[None]
    return (jnp.where(even, hs, hd), -jnp.where(even, hd, hs))


def factors(axis, cs):
    if axis == 0:
        return [cs.cx[n // 8] for n in range(16)]
    if axis == 1:
        return [float(2 * (n % 8) + 1) for n in range(16)]
    return [cs.ck] * 16


def times(rows, value):
    return jnp.stack([value[n] * rows[n] for n in range(16)])


def traces(fields, cs):
    out, inn, nexts = [], [], []
    for axis in range(3):
        low_p, high_p, next_p = SUMS[axis](fields[0], cs)
        low_u, high_u, next_u = SUMS[axis](fields[1 + axis], cs)
        out += [low_p - low_u, high_p + high_u]
        inn += [low_p + low_u, high_p - high_u]
        nexts.append((next_p, next_u))
    return (out, inn, nexts)


def outward_xy(fields, cs):
    out = []
    for side, sign in ((0, -1.0), (1, 1.0)):
        wave = fields[0] + fields[1] if side else fields[0] - fields[1]
        part = wave[0:8] + wave[8:16] if side else wave[0:8] - wave[8:16]
        part = part + pltpu.roll(part, 96, 2)
        out.append(part + pltpu.roll(part, 64, 2))
    for side in range(2):
        wave = fields[0] + fields[2] if side else fields[0] - fields[2]
        rows = []
        for il in range(2):
            even = (wave[8 * il] + wave[8 * il + 2]) + (wave[8 * il + 4] + wave[8 * il + 6])
            odd = (wave[8 * il + 1] + wave[8 * il + 3]) + (wave[8 * il + 5] + wave[8 * il + 7])
            rows.append(even + odd if side else even - odd)
        out.append(jnp.stack(rows))
    return out


def outside_waves(out, source, index, walls, cs, remote=None):
    result = []
    for f in range(6):
        src = row(source, f)
        own = row(walls, f).astype(jnp.float32)[None] * out[f]
        value = gather_rows(out[f ^ 1], cs.t * 32 + row(index, f))
        value = jnp.where((src == 5)[None], own, value)
        if f < 4:
            far = 0.0 if remote is None else remote[f]
            value = jnp.where((src == f + 1)[None], far, value)
        result.append(value)
    return result


def rates(out, inn, nexts, outside, cs):
    rate = [None] * 4
    for axis in range(3):
        low = outside[2 * axis] - inn[2 * axis]
        high = outside[2 * axis + 1] - inn[2 * axis + 1]
        gain_p, gain_u = spread(axis, (low + high) * 0.25, (high - low) * 0.25, cs)
        next_p, next_u = nexts[axis]
        fac = factors(axis, cs)
        part = times(fac, gain_p - next_u)
        rate[0] = part if axis == 0 else rate[0] + part
        rate[1 + axis] = times(fac, gain_u - next_p)
    return rate


def section_step(section, fields, stored, rate, step):
    stored = [SECTION_A[section] * stored[q] + step * rate[q] for q in range(4)]
    fields = [fields[q] + SECTION_B[section] * stored[q] for q in range(4)]
    return (fields, stored)


def pick(flag, first, second):
    return jnp.where(flag, first, second)


def even_index(axis_name):
    return jnp.full((8, 128), lax.axis_index(axis_name) % 2, jnp.int32) == 0


def read_tables(cs, scratch, orders, link_source, link_index, walls):
    order = row(lane_rows(scratch.at[0], orders, cs), 0)
    source = lane_rows(scratch.at[1], link_source, cs)
    index = lane_rows(scratch.at[2], link_index, cs)
    wall = lane_rows(scratch.at[3], walls, cs)
    return (order, source, index, wall)


def first_kernel(
    state_far, register_far, orders_far, source_far, index_far, walls_far, region_far, sub_far,
    fields_out, stored_out, tables_out, region_out, odd_out, even_out,
    state, register, orders, link_source, link_index, walls, send_region, send_sub, scratch, arrived,
):
    pairs = (
        (orders_far, orders), (source_far, link_source), (index_far, link_index), (walls_far, walls),
        (region_far, send_region), (sub_far, send_sub), (state_far, state), (register_far, register),
    )
    copies = [pltpu.make_async_copy(a, b, arrived.at[n]) for n, (a, b) in enumerate(pairs)]
    for copy in copies[6:] + copies[:6]:
        copy.start()
    cs = Consts()
    for copy in copies[:6]:
        copy.wait()
    order, source, index, wall = read_tables(cs, scratch, orders, link_source, link_index, walls)
    for n, table in enumerate((order, source, index, wall)):
        tables_out[8 * n : 8 * n + 8, :] = table
    region_list = lane_rows(scratch.at[4], send_region, cs)
    sub_list = lane_rows(scratch.at[5], send_sub, cs)
    keep = kept(cs, order)
    scale = jnp.stack([jnp.where(keep[n], w, 0.0) for n, w in enumerate(cs.weights(1))])
    step = jnp.stack([jnp.where(c, TIME_STEP, 0.0) for c in keep])
    copies[6].wait()
    fields = [load_field(state, q) * scale for q in range(4)]
    out, inn, nexts = traces(fields, cs)
    outside = outside_waves(out, source, index, wall, cs)
    rate = rates(out, inn, nexts, outside, cs)
    copies[7].wait()
    stored = [load_field(register, q) * scale for q in range(4)]
    fields, stored = section_step(0, fields, stored, rate, step)
    for q in range(4):
        fields_out[128 * q : 128 * q + 128, :] = fields[q].reshape(128, 128)
        stored_out[128 * q : 128 * q + 128, :] = stored[q].reshape(128, 128)
    later = outward_xy(fields, cs)

    places = order
    for f in range(4):
        place = jnp.where(row(source, f) == f + 1, row(index, f), -1)
        places = jnp.where(cs.k == f + 1, place, places)
    places = places.astype(jnp.float32)

    firsts = []
    for side in range(2):
        who = row(region_list, side)
        packed = jnp.zeros((8, 128), jnp.float32)
        for kind, waves in enumerate((out[side], later[side])):
            for j in range(8):
                packed = jnp.where(cs.lane // 8 == 8 * kind + j, lane_gather(waves[j], who), packed)
        region_out[16 * side : 16 * side + 8, :] = packed
        region_out[16 * side + 8 : 16 * side + 16, :] = lane_gather(places, who)
        firsts.append(packed)
    diagonal = jnp.where(cs.lane < 64, firsts[0], pltpu.roll(firsts[1], 64, 1))

    sides = []
    for side in range(2):
        who = (cs.lane // 8) % 4 * 32 + row(sub_list, side)
        packed = jnp.zeros((8, 128), jnp.float32)
        for kind, waves in enumerate((out[2 + side], later[2 + side])):
            for il in range(2):
                packed = jnp.where(cs.lane // 32 == 2 * kind + il, lane_gather(waves[il], who), packed)
        sides.append((packed, lane_gather(places, who)))
    even = even_index("sub")
    for n in range(2):
        low, high = sides[0][n], sides[1][n]
        at = 16 * n
        even_out[at : at + 8, :] = pick(even, high, low)
        odd_out[at : at + 8, :] = pick(even, low, high)
    even_out[8:16, :] = diagonal
    odd_out[8:16, :] = diagonal


def arrivals(even_ref, odd_ref, axis_name, rows):
    even = even_index(axis_name)
    below, above = [], []
    for n in range(rows):
        a, b = even_ref[8 * n : 8 * n + 8, :], odd_ref[8 * n : 8 * n + 8, :]
        if even_ref.shape[0] > odd_ref.shape[0]:
            other = odd_ref.shape[0] + 8 * n
            a = pick(even, even_ref[other : other + 8, :], a)
        below.append(pick(even, b, a))
        above.append(pick(even, a, b))
    return (below, above)


def second_kernel(region_base, sub_odd, sub_even, odd_out, even_out):
    cs = Consts()
    sub_below, sub_above = arrivals(sub_even, sub_odd, "sub", 2)
    target = (cs.lane // 8) % 8
    whole = []
    for side in range(2):
        packed = region_base[16 * side : 16 * side + 8, :]
        info = region_base[16 * side + 8 : 16 * side + 16, :].astype(jnp.int32)
        order = row(info, 0)
        added = jnp.zeros((8, 128), jnp.float32)
        for f, message in ((2, sub_below), (3, sub_above)):
            place = row(info, f + 1)
            at = jnp.maximum(place, 0)
            total = jnp.zeros((8, 128), jnp.float32)
            for i in range(8):
                got = lane_gather(message[0], 32 * (i % 2) + 8 * (i // 2) + at)
                got = jnp.where(i <= order, got, 0.0)
                total = total - got if side == 0 and i % 2 == 1 else total + got
            total = jnp.where(place >= 0, total, 0.0)
            if f == 2:
                total = jnp.where(target % 2 == 0, total, -total)
            added = added + total
        inside = jnp.maximum(target, cs.k) <= order
        inside = jnp.logical_and(inside, cs.lane >= 64)
        added = added * (CORNER * (2 * target + 1).astype(jnp.float32))
        packed = packed + jnp.where(inside, added, 0.0)
        below, above = sub_below[1], sub_above[1]
        if side == 0:
            relay = jnp.where(cs.lane < 64, below, pltpu.roll(above, 64, 1))
        else:
            relay = jnp.where(cs.lane < 64, pltpu.roll(below, 64, 1), above)
        whole.append((packed, relay))
    even = even_index("region")
    for n in range(2):
        low, high = whole[0][n], whole[1][n]
        even_out[8 * n : 8 * n + 8, :] = pick(even, high, low)
        odd_out[8 * n : 8 * n + 8, :] = pick(even, low, high)


def third_kernel(
    fields_in, stored_in, tables, sub_odd, sub_even, region_odd, region_even,
    state_far, register_far, state_out, register_out, left,
):
    cs = Consts()
    order, source, index, wall = [tables[8 * n : 8 * n + 8, :] for n in range(4)]
    sub_side = arrivals(sub_even, sub_odd, "sub", 3)
    region_side = arrivals(region_even, region_odd, "region", 2)
    keep = kept(cs, order)
    step = jnp.stack([jnp.where(c, TIME_STEP, 0.0) for c in keep])
    fields = [fields_in[128 * q : 128 * q + 128, :].reshape(16, 8, 128) for q in range(4)]
    stored = [stored_in[128 * q : 128 * q + 128, :].reshape(16, 8, 128) for q in range(4)]

    def arrived(kind, seconds):
        waves = []
        for side in range(2):
            at = 64 * kind + row(index, side) % 8
            message = region_side[side][0]
            waves.append(jnp.stack([lane_gather(message, at + 8 * j) for j in range(8)]))
        for side in range(2):
            at = 64 * kind + 8 * cs.t + row(index, 2 + side) % 8
            message = seconds[side] if kind else sub_side[side][0]
            waves.append(jnp.stack([lane_gather(message, at + 32 * il) for il in range(2)]))
        return waves

    first = arrived(0, None)
    first = [jnp.where((row(source, f) == f + 1)[None], first[f], 0.0) for f in range(4)]
    rate_p = None
    for axis in range(2):
        low, high = first[2 * axis], first[2 * axis + 1]
        gain_p, gain_u = spread(axis, (low + high) * 0.25, (high - low) * 0.25, cs)
        fac = factors(axis, cs)
        part = times(fac, gain_p)
        rate_p = part if axis == 0 else rate_p + part
        change = step * times(fac, gain_u)
        stored[1 + axis] = stored[1 + axis] + change
        fields[1 + axis] = fields[1 + axis] + SECTION_B[0] * change
    change = step * rate_p
    stored[0] = stored[0] + change
    fields[0] = fields[0] + SECTION_B[0] * change

    target = (cs.lane // 32) % 2 + 2 * ((cs.lane // 8) % 4)
    seconds = []
    for side in range(2):
        packed, _, info = sub_side[side]
        info = info.astype(jnp.int32)
        their_order = row(info, 0)
        added = jnp.zeros((8, 128), jnp.float32)
        for f in range(2):
            place = row(info, f + 1)
            at = 64 * side + jnp.maximum(place, 0) % 8
            relay = region_side[f][1]
            total = jnp.zeros((8, 128), jnp.float32)
            for j in range(8):
                got = jnp.where(j <= their_order, lane_gather(relay, at + 8 * j), 0.0)
                total = total - got if side == 1 and j % 2 == 1 else total + got
            total = jnp.where(place >= 0, total, 0.0)
            if f == 0:
                total = jnp.where(target % 2 == 0, total, -total)
            added = added + total
        inside = jnp.maximum(target, cs.k) <= their_order
        inside = jnp.logical_and(inside, cs.lane >= 64)
        added = added * (CORNER * (2 * target + 1).astype(jnp.float32))
        seconds.append(packed + jnp.where(inside, added, 0.0))

    out, inn, nexts = traces(fields, cs)
    outside = outside_waves(out, source, index, wall, cs, arrived(1, seconds))
    rate = rates(out, inn, nexts, outside, cs)
    fields, stored = section_step(1, fields, stored, rate, step)
    back = cs.weights(-1)
    copies = []
    for n, (values, ref, far) in enumerate(
        ((stored, register_out, register_far), (fields, state_out, state_far))
    ):
        for q in range(4):
            store_field(ref, q, values[q] * back)
        copies.append(pltpu.make_async_copy(ref, far, left.at[n]))
        copies[n].start()
    for copy in copies:
        copy.wait()


def swap(x, axis_name, parity, count):
    pairs = []
    for i in range(parity, count - 1, 2):
        pairs += [(i, i + 1), (i + 1, i)]
    return lax.ppermute(x, axis_name, pairs)


def gather_pairs(x, axis_name, count):
    groups = [[i, i + 1] for i in range(0, count, 2)]
    return lax.all_gather(x, axis_name, axis_index_groups=groups, tiled=True)


def call(kernel, outs, scratch, ins=None, out_space=pltpu.VMEM, kinds=None):
    kinds = [jnp.float32] * len(outs) if kinds is None else kinds
    space = pl.BlockSpec(memory_space=out_space)
    specs = {} if ins is None else dict(in_specs=[pl.BlockSpec(memory_space=pltpu.HBM)] * ins)
    return pl.pallas_call(
        kernel,
        out_shape=[jax.ShapeDtypeStruct((n, 128), kind) for n, kind in zip(outs, kinds)],
        out_specs=[space] * len(outs),
        scratch_shapes=scratch,
        compiler_params=pltpu.CompilerParams(vmem_limit_bytes=32 * 1024 * 1024),
        **specs,
    )


def body(counts, state, register, orders, link_source, link_index, walls, send_region, send_sub):
    def tiles(x):
        return x.reshape(32, 4, 4, 128).transpose(0, 2, 1, 3).reshape(512, 128)

    def untiles(x):
        return x.reshape(32, 4, 4, 128).transpose(0, 2, 1, 3).reshape(32, 4, 512)

    def held(x):
        return pltpu.with_memory_space_constraint(x, pltpu.HBM)

    whole = [pltpu.VMEM((512, 128), jnp.float32)] * 2
    small = [pltpu.VMEM(shape, jnp.int32) for shape in ((1, 32), (6, 32), (6, 32), (6, 32), (2, 8), (2, 8))]
    floats, ints = jnp.float32, jnp.int32
    fields, stored, tables, region_base, odd, even = call(
        first_kernel,
        (512, 512, 32, 32, 24, 24),
        whole + small + [pltpu.VMEM((6, 8, 128), jnp.int32), pltpu.SemaphoreType.DMA((8,))],
        ins=8,
        kinds=(floats, floats, ints, floats, floats, floats),
    )(
        held(tiles(state)), held(tiles(register)), held(orders.reshape(1, 32)), held(link_source.T),
        held(link_index.T), held(walls.T), held(send_region[0]), held(send_sub[0]),
    )
    sub_odd = swap(odd, "sub", 1, counts["sub"])
    sub_even = gather_pairs(even, "sub", counts["sub"])
    odd, even = call(second_kernel, (16, 16), [])(region_base, sub_odd, sub_even)
    region_odd = swap(odd, "region", 1, counts["region"])
    region_even = gather_pairs(even, "region", counts["region"])
    state, register = call(
        third_kernel, (512, 512), whole + [pltpu.SemaphoreType.DMA((2,))], out_space=pltpu.HBM
    )(fields, stored, tables, sub_odd, sub_even, region_odd, region_even)
    return (untiles(state), untiles(register))


def solution(mesh):
    both = P(("region", "sub"))
    return jax.shard_map(
        functools.partial(body, dict(mesh.shape)),
        mesh=mesh,
        in_specs=(both,) * 8,
        out_specs=(both, both),
        check_vma=False,
    )
```

```python
import functools
import math

import jax
import jax.numpy as jnp
from jax import lax
from jax.experimental import pallas as pl
from jax.experimental.pallas import tpu as pltpu
from jax.sharding import PartitionSpec as P

SECTION_A = (-567301805773.0 / 1357537059087.0, -2404267990393.0 / 2016746695238.0)
SECTION_B = (5161836677717.0 / 13612068292357.0, 1720146321549.0 / 2090206949498.0)
TIME_STEP = 0.02
CORNER = TIME_STEP * SECTION_B[0] * 0.25


def lane_gather(x, idx):
    dims = lax.GatherDimensionNumbers(
        offset_dims=(),
        collapsed_slice_dims=(1,),
        start_index_map=(1,),
        operand_batching_dims=(0,),
        start_indices_batching_dims=(0,),
    )
    return lax.gather(
        x, idx[..., None], dims, slice_sizes=(1, 1), mode=lax.GatherScatterMode.PROMISE_IN_BOUNDS
    )


def gather_rows(x, idx):
    return jnp.stack([lane_gather(x[n], idx) for n in range(x.shape[0])])


class Consts:
    def __init__(self):
        self.lane = lax.broadcasted_iota(jnp.int32, (8, 128), 1)
        self.k = lax.broadcasted_iota(jnp.int32, (8, 128), 0)
        self.t = self.lane // 32
        self.even_k = (self.k % 2) == 0
        self.sgn_k = jnp.where(self.even_k, 1.0, -1.0)
        self.ck = (2 * self.k + 1).astype(jnp.float32)
        self.cx = [(4 * self.t + 2 * il + 1).astype(jnp.float32) for il in range(2)]

    def table(self, index, values):
        out = jnp.full((8, 128), values[0], jnp.float32)
        for n in range(1, len(values)):
            out = jnp.where(index == n, values[n], out)
        return out

    def weights(self, power):
        root = [math.sqrt((2 * n + 1) / 2.0) ** power for n in range(8)]
        along_k = self.table(self.k, root)
        rows = []
        for il in range(2):
            base = along_k * self.table(self.t, root[il::2])
            rows += [base * root[j] for j in range(8)]
        return jnp.stack(rows)


def kept(cs, order):
    rows = []
    for il in range(2):
        inner = jnp.maximum(cs.k, 2 * cs.t + il)
        rows += [jnp.maximum(inner, j) <= order for j in range(8)]
    return rows


def load_field(ref, q):
    rows = [ref[pl.ds(4 * t + q, 32, stride=16), :] for t in range(4)]
    return jnp.concatenate(rows, axis=0).T.reshape(16, 8, 128)


def store_field(ref, q, value):
    turned = value.reshape(128, 128).T
    for t in range(4):
        ref[pl.ds(4 * t + q, 32, stride=16), :] = turned[32 * t : 32 * t + 32]


def lane_rows(scratch, ref, cs):
    rows, width = ref.shape
    scratch[0:rows, 0:width] = ref[...]
    return lane_gather(scratch[...], cs.lane % width)


def row(x, n):
    return jnp.broadcast_to(x[n : n + 1, :], (8, 128))


def sums_x(b, cs):
    lane = cs.lane[None]
    r1, r2, r3 = [pltpu.roll(b, n, 2) for n in (96, 64, 32)]
    above = jnp.where(lane < 96, r1, 0.0) + (
        jnp.where(lane < 64, r2, 0.0) + jnp.where(lane < 32, r3, 0.0)
    )
    tot = (b + r1) + (r2 + r3)
    nxt = jnp.concatenate([b[8:16] + above[8:16], above[0:8]], axis=0)
    return (tot[0:8] - tot[8:16], tot[0:8] + tot[8:16], nxt)


def sums_y(b, cs):
    low, high, nxt = [], [], []
    for il in range(2):
        s = [b[8 * il + j] for j in range(8)]
        for j in range(5, -1, -1):
            s[j] = s[j] + s[j + 2]
        low.append(s[0] - s[1])
        high.append(s[0] + s[1])
        nxt += s[1:] + [jnp.zeros_like(s[0])]
    return (jnp.stack(low), jnp.stack(high), jnp.stack(nxt))


def sums_z(b, cs):
    k = cs.k[None]
    r1 = pltpu.roll(b, 6, 1)
    u = b + jnp.where(k < 6, r1, 0.0)
    uc = b + r1
    s = u + jnp.where(k < 4, pltpu.roll(u, 4, 1), 0.0)
    tot = uc + pltpu.roll(uc, 4, 1)
    other = pltpu.roll(tot, 1, 1)
    return (cs.sgn_k[None] * (tot - other), tot + other, jnp.where(k < 7, pltpu.roll(s, 7, 1), 0.0))


SUMS = (sums_x, sums_y, sums_z)


def spread(axis, hs, hd, cs):
    if axis == 0:
        return (jnp.concatenate([hs, hd]), jnp.concatenate([-hd, -hs]))
    if axis == 1:
        gain_p = jnp.stack([(hs, hd)[j % 2][il] for il in range(2) for j in range(8)])
        gain_u = jnp.stack([-(hd, hs)[j % 2][il] for il in range(2) for j in range(8)])
        return (gain_p, gain_u)
    even = cs.even_k[None]
    return (jnp.where(even, hs, hd), -jnp.where(even, hd, hs))


def factors(axis, cs):
    if axis == 0:
        return [cs.cx[n // 8] for n in range(16)]
    if axis == 1:
        return [float(2 * (n % 8) + 1) for n in range(16)]
    return [cs.ck] * 16


def times(rows, value):
    return jnp.stack([value[n] * rows[n] for n in range(16)])


def traces(fields, cs):
    out, inn, nexts = [], [], []
    for axis in range(3):
        low_p, high_p, next_p = SUMS[axis](fields[0], cs)
        low_u, high_u, next_u = SUMS[axis](fields[1 + axis], cs)
        out += [low_p - low_u, high_p + high_u]
        inn += [low_p + low_u, high_p - high_u]
        nexts.append((next_p, next_u))
    return (out, inn, nexts)


def outward_xy(fields, cs):
    out = []
    for side, sign in ((0, -1.0), (1, 1.0)):
        wave = fields[0] + fields[1] if side else fields[0] - fields[1]
        part = wave[0:8] + wave[8:16] if side else wave[0:8] - wave[8:16]
        part = part + pltpu.roll(part, 96, 2)
        out.append(part + pltpu.roll(part, 64, 2))
    for side in range(2):
        wave = fields[0] + fields[2] if side else fields[0] - fields[2]
        rows = []
        for il in range(2):
            even = (wave[8 * il] + wave[8 * il + 2]) + (wave[8 * il + 4] + wave[8 * il + 6])
            odd = (wave[8 * il + 1] + wave[8 * il + 3]) + (wave[8 * il + 5] + wave[8 * il + 7])
            rows.append(even + odd if side else even - odd)
        out.append(jnp.stack(rows))
    return out


def outside_waves(out, source, index, walls, cs, remote=None):
    result = []
    for f in range(6):
        src = row(source, f)
        own = row(walls, f).astype(jnp.float32)[None] * out[f]
        value = gather_rows(out[f ^ 1], cs.t * 32 + row(index, f))
        value = jnp.where((src == 5)[None], own, value)
        if f < 4:
            far = 0.0 if remote is None else remote[f]
            value = jnp.where((src == f + 1)[None], far, value)
        result.append(value)
    return result


def rates(out, inn, nexts, outside, cs):
    rate = [None] * 4
    for axis in range(3):
        low = outside[2 * axis] - inn[2 * axis]
        high = outside[2 * axis + 1] - inn[2 * axis + 1]
        gain_p, gain_u = spread(axis, (low + high) * 0.25, (high - low) * 0.25, cs)
        next_p, next_u = nexts[axis]
        fac = factors(axis, cs)
        part = times(fac, gain_p - next_u)
        rate[0] = part if axis == 0 else rate[0] + part
        rate[1 + axis] = times(fac, gain_u - next_p)
    return rate


def section_step(section, fields, stored, rate, step):
    stored = [SECTION_A[section] * stored[q] + step * rate[q] for q in range(4)]
    fields = [fields[q] + SECTION_B[section] * stored[q] for q in range(4)]
    return (fields, stored)


def pick(flag, first, second):
    return jnp.where(flag, first, second)


def even_index(axis_name):
    return jnp.full((8, 128), lax.axis_index(axis_name) % 2, jnp.int32) == 0


def read_tables(cs, scratch, orders, link_source, link_index, walls):
    order = row(lane_rows(scratch.at[0], orders, cs), 0)
    source = lane_rows(scratch.at[1], link_source, cs)
    index = lane_rows(scratch.at[2], link_index, cs)
    wall = lane_rows(scratch.at[3], walls, cs)
    return (order, source, index, wall)


def first_kernel(
    state_far, register_far, orders_far, source_far, index_far, walls_far, region_far, sub_far,
    fields_out, stored_out, tables_out, region_out, odd_out, even_out,
    state, register, orders, link_source, link_index, walls, send_region, send_sub, scratch, arrived,
):
    pairs = (
        (orders_far, orders), (source_far, link_source), (index_far, link_index), (walls_far, walls),
        (region_far, send_region), (sub_far, send_sub), (state_far, state), (register_far, register),
    )
    copies = [pltpu.make_async_copy(a, b, arrived.at[n]) for n, (a, b) in enumerate(pairs)]
    for copy in copies[6:] + copies[:6]:
        copy.start()
    cs = Consts()
    for copy in copies[:6]:
        copy.wait()
    order, source, index, wall = read_tables(cs, scratch, orders, link_source, link_index, walls)
    for n, table in enumerate((order, source, index, wall)):
        tables_out[8 * n : 8 * n + 8, :] = table
    region_list = lane_rows(scratch.at[4], send_region, cs)
    sub_list = lane_rows(scratch.at[5], send_sub, cs)
    keep = kept(cs, order)
    scale = jnp.stack([jnp.where(keep[n], w, 0.0) for n, w in enumerate(cs.weights(1))])
    step = jnp.stack([jnp.where(c, TIME_STEP, 0.0) for c in keep])
    copies[6].wait()
    fields = [load_field(state, q) * scale for q in range(4)]
    out, inn, nexts = traces(fields, cs)
    outside = outside_waves(out, source, index, wall, cs)
    rate = rates(out, inn, nexts, outside, cs)
    copies[7].wait()
    stored = [load_field(register, q) * scale for q in range(4)]
    fields, stored = section_step(0, fields, stored, rate, step)
    for q in range(4):
        fields_out[128 * q : 128 * q + 128, :] = fields[q].reshape(128, 128)
        stored_out[128 * q : 128 * q + 128, :] = stored[q].reshape(128, 128)
    later = outward_xy(fields, cs)

    places = order
    for f in range(4):
        place = jnp.where(row(source, f) == f + 1, row(index, f), -1)
        places = jnp.where(cs.k == f + 1, place, places)
    places = places.astype(jnp.float32)

    firsts = []
    for side in range(2):
        who = row(region_list, side)
        packed = jnp.zeros((8, 128), jnp.float32)
        for kind, waves in enumerate((out[side], later[side])):
            for j in range(8):
                packed = jnp.where(cs.lane // 8 == 8 * kind + j, lane_gather(waves[j], who), packed)
        region_out[16 * side : 16 * side + 8, :] = packed
        region_out[16 * side + 8 : 16 * side + 16, :] = lane_gather(places, who)
        firsts.append(packed)
    diagonal = jnp.where(cs.lane < 64, firsts[0], pltpu.roll(firsts[1], 64, 1))

    sides = []
    for side in range(2):
        who = (cs.lane // 8) % 4 * 32 + row(sub_list, side)
        packed = jnp.zeros((8, 128), jnp.float32)
        for kind, waves in enumerate((out[2 + side], later[2 + side])):
            for il in range(2):
                packed = jnp.where(cs.lane // 32 == 2 * kind + il, lane_gather(waves[il], who), packed)
        sides.append((packed, lane_gather(places, who)))
    even = even_index("sub")
    for n in range(2):
        low, high = sides[0][n], sides[1][n]
        at = 16 * n
        even_out[at : at + 8, :] = pick(even, high, low)
        odd_out[at : at + 8, :] = pick(even, low, high)
    even_out[8:16, :] = diagonal
    odd_out[8:16, :] = diagonal


def arrivals(even_ref, odd_ref, axis_name, rows):
    even = even_index(axis_name)
    below, above = [], []
    for n in range(rows):
        a, b = even_ref[8 * n : 8 * n + 8, :], odd_ref[8 * n : 8 * n + 8, :]
        if even_ref.shape[0] > odd_ref.shape[0]:
            other = odd_ref.shape[0] + 8 * n
            a = pick(even, even_ref[other : other + 8, :], a)
        below.append(pick(even, b, a))
        above.append(pick(even, a, b))
    return (below, above)


def region_message(region_base, sub_odd, sub_even, out, down, cs):
    sub_below, sub_above = arrivals(sub_even, sub_odd, "sub", 2)
    target = (cs.lane // 8) % 8
    packed = pick(down, region_base[0:8, :], region_base[16:24, :])
    info = pick(down, region_base[8:16, :], region_base[24:32, :]).astype(jnp.int32)
    order = row(info, 0)
    sign = jnp.where(down, -1.0, 1.0)
    added = jnp.zeros((8, 128), jnp.float32)
    for f, message in ((2, sub_below), (3, sub_above)):
        place = row(info, f + 1)
        at = jnp.maximum(place, 0) % 8
        sums = [jnp.zeros((8, 128), jnp.float32)] * 2
        for i in range(8):
            got = lane_gather(message[0], 32 * (i % 2) + 8 * (i // 2) + at)
            sums[i % 2] = sums[i % 2] + jnp.where(i <= order, got, 0.0)
        total = jnp.where(place >= 0, sums[0] + sign * sums[1], 0.0)
        if f == 2:
            total = jnp.where(target % 2 == 0, total, -total)
        added = added + total
    inside = jnp.logical_and(jnp.maximum(target, cs.k) <= order, cs.lane >= 64)
    added = added * (CORNER * (2 * target + 1).astype(jnp.float32))
    out[0:8, :] = packed + jnp.where(inside, added, 0.0)
    below, above = sub_below[1], sub_above[1]
    out[8:16, :] = pick(
        down,
        jnp.where(cs.lane < 64, below, pltpu.roll(above, 64, 1)),
        jnp.where(cs.lane < 64, pltpu.roll(below, 64, 1), above),
    )


def second_kernel(region_base, sub_odd, sub_even, odd_out):
    region_message(region_base, sub_odd, sub_even, odd_out, even_index("region"), Consts())


def flight_kernel(region_base, sub_odd, sub_even, after, even_out):
    del after
    down = jnp.logical_not(even_index("region"))
    region_message(region_base, sub_odd, sub_even, even_out, down, Consts())


def third_kernel(
    fields_in, stored_in, tables, sub_odd, sub_even, region_odd, region_even,
    state_far, register_far, state_out, register_out, left,
):
    cs = Consts()
    order, source, index, wall = [tables[8 * n : 8 * n + 8, :] for n in range(4)]
    sub_side = arrivals(sub_even, sub_odd, "sub", 3)
    region_side = arrivals(region_even, region_odd, "region", 2)
    keep = kept(cs, order)
    step = jnp.stack([jnp.where(c, TIME_STEP, 0.0) for c in keep])
    fields = [fields_in[128 * q : 128 * q + 128, :].reshape(16, 8, 128) for q in range(4)]
    stored = [stored_in[128 * q : 128 * q + 128, :].reshape(16, 8, 128) for q in range(4)]

    def arrived(kind, seconds):
        waves = []
        for side in range(2):
            at = 64 * kind + row(index, side) % 8
            message = region_side[side][0]
            waves.append(jnp.stack([lane_gather(message, at + 8 * j) for j in range(8)]))
        for side in range(2):
            at = 64 * kind + 8 * cs.t + row(index, 2 + side) % 8
            message = seconds[side] if kind else sub_side[side][0]
            waves.append(jnp.stack([lane_gather(message, at + 32 * il) for il in range(2)]))
        return waves

    first = arrived(0, None)
    first = [jnp.where((row(source, f) == f + 1)[None], first[f], 0.0) for f in range(4)]
    rate_p = None
    for axis in range(2):
        low, high = first[2 * axis], first[2 * axis + 1]
        gain_p, gain_u = spread(axis, (low + high) * 0.25, (high - low) * 0.25, cs)
        fac = factors(axis, cs)
        part = times(fac, gain_p)
        rate_p = part if axis == 0 else rate_p + part
        change = step * times(fac, gain_u)
        stored[1 + axis] = stored[1 + axis] + change
        fields[1 + axis] = fields[1 + axis] + SECTION_B[0] * change
    change = step * rate_p
    stored[0] = stored[0] + change
    fields[0] = fields[0] + SECTION_B[0] * change

    target = (cs.lane // 32) % 2 + 2 * ((cs.lane // 8) % 4)
    seconds = []
    for side in range(2):
        packed, _, info = sub_side[side]
        info = info.astype(jnp.int32)
        their_order = row(info, 0)
        added = jnp.zeros((8, 128), jnp.float32)
        for f in range(2):
            place = row(info, f + 1)
            at = 64 * side + jnp.maximum(place, 0) % 8
            relay = region_side[f][1]
            total = jnp.zeros((8, 128), jnp.float32)
            for j in range(8):
                got = jnp.where(j <= their_order, lane_gather(relay, at + 8 * j), 0.0)
                total = total - got if side == 1 and j % 2 == 1 else total + got
            total = jnp.where(place >= 0, total, 0.0)
            if f == 0:
                total = jnp.where(target % 2 == 0, total, -total)
            added = added + total
        inside = jnp.maximum(target, cs.k) <= their_order
        inside = jnp.logical_and(inside, cs.lane >= 64)
        added = added * (CORNER * (2 * target + 1).astype(jnp.float32))
        seconds.append(packed + jnp.where(inside, added, 0.0))

    out, inn, nexts = traces(fields, cs)
    outside = outside_waves(out, source, index, wall, cs, arrived(1, seconds))
    rate = rates(out, inn, nexts, outside, cs)
    fields, stored = section_step(1, fields, stored, rate, step)
    back = cs.weights(-1)
    copies = []
    for n, (values, ref, far) in enumerate(
        ((stored, register_out, register_far), (fields, state_out, state_far))
    ):
        for q in range(4):
            store_field(ref, q, values[q] * back)
        copies.append(pltpu.make_async_copy(ref, far, left.at[n]))
        copies[n].start()
    for copy in copies:
        copy.wait()


def swap(x, axis_name, parity, count):
    pairs = []
    for i in range(parity, count - 1, 2):
        pairs += [(i, i + 1), (i + 1, i)]
    return lax.ppermute(x, axis_name, pairs)


def gather_pairs(x, axis_name, count):
    groups = [[i, i + 1] for i in range(0, count, 2)]
    return lax.all_gather(x, axis_name, axis_index_groups=groups, tiled=True)


def call(kernel, outs, scratch, ins=None, out_space=pltpu.VMEM, kinds=None):
    kinds = [jnp.float32] * len(outs) if kinds is None else kinds
    space = pl.BlockSpec(memory_space=out_space)
    specs = {} if ins is None else dict(in_specs=[pl.BlockSpec(memory_space=pltpu.HBM)] * ins)
    return pl.pallas_call(
        kernel,
        out_shape=[jax.ShapeDtypeStruct((n, 128), kind) for n, kind in zip(outs, kinds)],
        out_specs=[space] * len(outs),
        scratch_shapes=scratch,
        compiler_params=pltpu.CompilerParams(vmem_limit_bytes=32 * 1024 * 1024),
        **specs,
    )


def body(counts, state, register, orders, link_source, link_index, walls, send_region, send_sub):
    def tiles(x):
        return x.reshape(32, 4, 4, 128).transpose(0, 2, 1, 3).reshape(512, 128)

    def untiles(x):
        return x.reshape(32, 4, 4, 128).transpose(0, 2, 1, 3).reshape(32, 4, 512)

    def held(x):
        return pltpu.with_memory_space_constraint(x, pltpu.HBM)

    whole = [pltpu.VMEM((512, 128), jnp.float32)] * 2
    small = [pltpu.VMEM(shape, jnp.int32) for shape in ((1, 32), (6, 32), (6, 32), (6, 32), (2, 8), (2, 8))]
    floats, ints = jnp.float32, jnp.int32
    fields, stored, tables, region_base, odd, even = call(
        first_kernel,
        (512, 512, 32, 32, 24, 24),
        whole + small + [pltpu.VMEM((6, 8, 128), jnp.int32), pltpu.SemaphoreType.DMA((8,))],
        ins=8,
        kinds=(floats, floats, ints, floats, floats, floats),
    )(
        held(tiles(state)), held(tiles(register)), held(orders.reshape(1, 32)), held(link_source.T),
        held(link_index.T), held(walls.T), held(send_region[0]), held(send_sub[0]),
    )
    sub_odd = swap(odd, "sub", 1, counts["sub"])
    sub_even = gather_pairs(even, "sub", counts["sub"])
    (odd,) = call(second_kernel, (16,), [])(region_base, sub_odd, sub_even)
    region_odd = swap(odd, "region", 1, counts["region"])
    (even,) = call(flight_kernel, (16,), [])(region_base, sub_odd, sub_even, odd)
    region_even = gather_pairs(even, "region", counts["region"])
    state, register = call(
        third_kernel, (512, 512), whole + [pltpu.SemaphoreType.DMA((2,))], out_space=pltpu.HBM
    )(fields, stored, tables, sub_odd, sub_even, region_odd, region_even)
    return (untiles(state), untiles(register))


def solution(mesh):
    both = P(("region", "sub"))
    return jax.shard_map(
        functools.partial(body, dict(mesh.shape)),
        mesh=mesh,
        in_specs=(both,) * 8,
        out_specs=(both, both),
        check_vma=False,
    )
```

```python
import functools
import math

import jax
import jax.numpy as jnp
from jax import lax
from jax.experimental import pallas as pl
from jax.experimental.pallas import tpu as pltpu
from jax.sharding import PartitionSpec as P

SECTION_A = (-567301805773.0 / 1357537059087.0, -2404267990393.0 / 2016746695238.0)
SECTION_B = (5161836677717.0 / 13612068292357.0, 1720146321549.0 / 2090206949498.0)
TIME_STEP = 0.02
CORNER = TIME_STEP * SECTION_B[0] * 0.25


def lane_gather(x, idx):
    dims = lax.GatherDimensionNumbers(
        offset_dims=(),
        collapsed_slice_dims=(1,),
        start_index_map=(1,),
        operand_batching_dims=(0,),
        start_indices_batching_dims=(0,),
    )
    return lax.gather(
        x, idx[..., None], dims, slice_sizes=(1, 1), mode=lax.GatherScatterMode.PROMISE_IN_BOUNDS
    )


def gather_rows(x, idx):
    return jnp.stack([lane_gather(x[n], idx) for n in range(x.shape[0])])


class Consts:
    def __init__(self):
        self.lane = lax.broadcasted_iota(jnp.int32, (8, 128), 1)
        self.k = lax.broadcasted_iota(jnp.int32, (8, 128), 0)
        self.t = self.lane // 32
        self.even_k = (self.k % 2) == 0
        self.sgn_k = jnp.where(self.even_k, 1.0, -1.0)
        self.ck = (2 * self.k + 1).astype(jnp.float32)
        self.cx = [(4 * self.t + 2 * il + 1).astype(jnp.float32) for il in range(2)]

    def table(self, index, values):
        out = jnp.full((8, 128), values[0], jnp.float32)
        for n in range(1, len(values)):
            out = jnp.where(index == n, values[n], out)
        return out

    def weights(self, power):
        root = [math.sqrt((2 * n + 1) / 2.0) ** power for n in range(8)]
        along_k = self.table(self.k, root)
        rows = []
        for il in range(2):
            base = along_k * self.table(self.t, root[il::2])
            rows += [base * root[j] for j in range(8)]
        return jnp.stack(rows)


def kept(cs, order):
    rows = []
    for il in range(2):
        inner = jnp.maximum(cs.k, 2 * cs.t + il)
        rows += [jnp.maximum(inner, j) <= order for j in range(8)]
    return rows


def load_field(ref, q):
    rows = [ref[pl.ds(4 * t + q, 32, stride=16), :] for t in range(4)]
    return jnp.concatenate(rows, axis=0).T.reshape(16, 8, 128)


def store_field(ref, q, value):
    turned = value.reshape(128, 128).T
    for t in range(4):
        ref[pl.ds(4 * t + q, 32, stride=16), :] = turned[32 * t : 32 * t + 32]


def lane_rows(scratch, ref, cs):
    rows, width = ref.shape
    scratch[0:rows, 0:width] = ref[...]
    return lane_gather(scratch[...], cs.lane % width)


def row(x, n):
    return jnp.broadcast_to(x[n : n + 1, :], (8, 128))


def sums_x(b, cs):
    lane = cs.lane[None]
    r1, r2, r3 = [pltpu.roll(b, n, 2) for n in (96, 64, 32)]
    above = jnp.where(lane < 96, r1, 0.0) + (
        jnp.where(lane < 64, r2, 0.0) + jnp.where(lane < 32, r3, 0.0)
    )
    tot = (b + r1) + (r2 + r3)
    nxt = jnp.concatenate([b[8:16] + above[8:16], above[0:8]], axis=0)
    return (tot[0:8] - tot[8:16], tot[0:8] + tot[8:16], nxt)


def sums_y(b, cs):
    low, high, nxt = [], [], []
    for il in range(2):
        s = [b[8 * il + j] for j in range(8)]
        for j in range(5, -1, -1):
            s[j] = s[j] + s[j + 2]
        low.append(s[0] - s[1])
        high.append(s[0] + s[1])
        nxt += s[1:] + [jnp.zeros_like(s[0])]
    return (jnp.stack(low), jnp.stack(high), jnp.stack(nxt))


def sums_z(b, cs):
    k = cs.k[None]
    r1 = pltpu.roll(b, 6, 1)
    u = b + jnp.where(k < 6, r1, 0.0)
    uc = b + r1
    s = u + jnp.where(k < 4, pltpu.roll(u, 4, 1), 0.0)
    tot = uc + pltpu.roll(uc, 4, 1)
    other = pltpu.roll(tot, 1, 1)
    return (cs.sgn_k[None] * (tot - other), tot + other, jnp.where(k < 7, pltpu.roll(s, 7, 1), 0.0))


SUMS = (sums_x, sums_y, sums_z)


def spread(axis, hs, hd, cs):
    if axis == 0:
        return (jnp.concatenate([hs, hd]), jnp.concatenate([-hd, -hs]))
    if axis == 1:
        gain_p = jnp.stack([(hs, hd)[j % 2][il] for il in range(2) for j in range(8)])
        gain_u = jnp.stack([-(hd, hs)[j % 2][il] for il in range(2) for j in range(8)])
        return (gain_p, gain_u)
    even = cs.even_k[None]
    return (jnp.where(even, hs, hd), -jnp.where(even, hd, hs))


def factors(axis, cs):
    if axis == 0:
        return [cs.cx[n // 8] for n in range(16)]
    if axis == 1:
        return [float(2 * (n % 8) + 1) for n in range(16)]
    return [cs.ck] * 16


def times(rows, value):
    return jnp.stack([value[n] * rows[n] for n in range(16)])


def traces(fields, cs):
    out, inn, nexts = [], [], []
    for axis in range(3):
        low_p, high_p, next_p = SUMS[axis](fields[0], cs)
        low_u, high_u, next_u = SUMS[axis](fields[1 + axis], cs)
        out += [low_p - low_u, high_p + high_u]
        inn += [low_p + low_u, high_p - high_u]
        nexts.append((next_p, next_u))
    return (out, inn, nexts)


def outward_xy(fields, cs):
    out = []
    for side, sign in ((0, -1.0), (1, 1.0)):
        wave = fields[0] + fields[1] if side else fields[0] - fields[1]
        part = wave[0:8] + wave[8:16] if side else wave[0:8] - wave[8:16]
        part = part + pltpu.roll(part, 96, 2)
        out.append(part + pltpu.roll(part, 64, 2))
    for side in range(2):
        wave = fields[0] + fields[2] if side else fields[0] - fields[2]
        rows = []
        for il in range(2):
            even = (wave[8 * il] + wave[8 * il + 2]) + (wave[8 * il + 4] + wave[8 * il + 6])
            odd = (wave[8 * il + 1] + wave[8 * il + 3]) + (wave[8 * il + 5] + wave[8 * il + 7])
            rows.append(even + odd if side else even - odd)
        out.append(jnp.stack(rows))
    return out


def outside_waves(out, source, index, walls, cs, remote=None):
    result = []
    for f in range(6):
        src = row(source, f)
        own = row(walls, f).astype(jnp.float32)[None] * out[f]
        value = gather_rows(out[f ^ 1], cs.t * 32 + row(index, f))
        value = jnp.where((src == 5)[None], own, value)
        if f < 4:
            far = 0.0 if remote is None else remote[f]
            value = jnp.where((src == f + 1)[None], far, value)
        result.append(value)
    return result


def rates(out, inn, nexts, outside, cs):
    rate = [None] * 4
    for axis in range(3):
        low = outside[2 * axis] - inn[2 * axis]
        high = outside[2 * axis + 1] - inn[2 * axis + 1]
        gain_p, gain_u = spread(axis, (low + high) * 0.25, (high - low) * 0.25, cs)
        next_p, next_u = nexts[axis]
        fac = factors(axis, cs)
        part = times(fac, gain_p - next_u)
        rate[0] = part if axis == 0 else rate[0] + part
        rate[1 + axis] = times(fac, gain_u - next_p)
    return rate


def section_step(section, fields, stored, rate, step):
    stored = [SECTION_A[section] * stored[q] + step * rate[q] for q in range(4)]
    fields = [fields[q] + SECTION_B[section] * stored[q] for q in range(4)]
    return (fields, stored)


def pick(flag, first, second):
    return jnp.where(flag, first, second)


def mode_sum(message, at, low_step, high_step, order, alternate, cs):
    half = cs.lane // 64
    total = jnp.zeros((8, 128), jnp.float32)
    for n in range(4):
        got = lane_gather(message, at + (low_step * half + high_step * n))
        total = total + jnp.where(2 * n + half <= order, got, 0.0)
    even = pltpu.roll(total, 64, 1)
    return even - total if alternate else even + total


def even_index(axis_name):
    return jnp.full((8, 128), lax.axis_index(axis_name) % 2, jnp.int32) == 0


def read_tables(cs, scratch, orders, link_source, link_index, walls):
    order = row(lane_rows(scratch.at[0], orders, cs), 0)
    source = lane_rows(scratch.at[1], link_source, cs)
    index = lane_rows(scratch.at[2], link_index, cs)
    wall = lane_rows(scratch.at[3], walls, cs)
    return (order, source, index, wall)


def first_kernel(
    state_far, register_far, orders_far, source_far, index_far, walls_far, region_far, sub_far,
    fields_out, stored_out, tables_out, region_out, odd_out, even_out,
    state, register, orders, link_source, link_index, walls, send_region, send_sub, scratch, arrived,
):
    pairs = (
        (orders_far, orders), (source_far, link_source), (index_far, link_index), (walls_far, walls),
        (region_far, send_region), (sub_far, send_sub), (state_far, state), (register_far, register),
    )
    copies = [pltpu.make_async_copy(a, b, arrived.at[n]) for n, (a, b) in enumerate(pairs)]
    for copy in copies[6:] + copies[:6]:
        copy.start()
    cs = Consts()
    for copy in copies[:6]:
        copy.wait()
    order, source, index, wall = read_tables(cs, scratch, orders, link_source, link_index, walls)
    for n, table in enumerate((order, source, index, wall)):
        tables_out[8 * n : 8 * n + 8, :] = table
    region_list = lane_rows(scratch.at[4], send_region, cs)
    sub_list = lane_rows(scratch.at[5], send_sub, cs)
    keep = kept(cs, order)
    scale = jnp.stack([jnp.where(keep[n], w, 0.0) for n, w in enumerate(cs.weights(1))])
    step = jnp.stack([jnp.where(c, TIME_STEP, 0.0) for c in keep])
    copies[6].wait()
    fields = [load_field(state, q) * scale for q in range(4)]
    out, inn, nexts = traces(fields, cs)
    outside = outside_waves(out, source, index, wall, cs)
    rate = rates(out, inn, nexts, outside, cs)
    copies[7].wait()
    stored = [load_field(register, q) * scale for q in range(4)]
    fields, stored = section_step(0, fields, stored, rate, step)
    for q in range(4):
        fields_out[128 * q : 128 * q + 128, :] = fields[q].reshape(128, 128)
        stored_out[128 * q : 128 * q + 128, :] = stored[q].reshape(128, 128)
    later = outward_xy(fields, cs)

    places = order
    for f in range(4):
        place = jnp.where(row(source, f) == f + 1, row(index, f), -1)
        places = jnp.where(cs.k == f + 1, place, places)
    places = places.astype(jnp.float32)

    firsts = []
    for side in range(2):
        who = row(region_list, side)
        packed = jnp.zeros((8, 128), jnp.float32)
        first, second = out[side], later[side]
        group = cs.lane // 64 + 2 * ((cs.lane // 8) % 2)
        for n in range(4):
            low = jnp.where(cs.t == 0, first[2 * n], second[2 * n])
            high = jnp.where(cs.t == 2, first[2 * n + 1], second[2 * n + 1])
            got = lane_gather(jnp.where(cs.t < 2, low, high), 32 * group + who)
            packed = jnp.where((cs.lane // 16) % 4 == n, got, packed)
        region_out[16 * side : 16 * side + 8, :] = packed
        region_out[16 * side + 8 : 16 * side + 16, :] = lane_gather(places, who)
        firsts.append(packed)
    diagonal = jnp.where(cs.lane < 64, firsts[0], pltpu.roll(firsts[1], 64, 1))

    sides = []
    for side in range(2):
        who = (cs.lane // 8) % 4 * 32 + row(sub_list, side)
        packed = jnp.zeros((8, 128), jnp.float32)
        for kind, waves in enumerate((out[2 + side], later[2 + side])):
            for il in range(2):
                packed = jnp.where(cs.lane // 32 == 2 * kind + il, lane_gather(waves[il], who), packed)
        sides.append((packed, lane_gather(places, who)))
    even = even_index("sub")
    for n in range(2):
        low, high = sides[0][n], sides[1][n]
        at = 16 * n
        even_out[at : at + 8, :] = pick(even, high, low)
        odd_out[at : at + 8, :] = pick(even, low, high)
    even_out[8:16, :] = diagonal
    odd_out[8:16, :] = diagonal


def arrivals(even_ref, odd_ref, axis_name, rows):
    even = even_index(axis_name)
    below, above = [], []
    for n in range(rows):
        a, b = even_ref[8 * n : 8 * n + 8, :], odd_ref[8 * n : 8 * n + 8, :]
        if even_ref.shape[0] > odd_ref.shape[0]:
            other = odd_ref.shape[0] + 8 * n
            a = pick(even, even_ref[other : other + 8, :], a)
        below.append(pick(even, b, a))
        above.append(pick(even, a, b))
    return (below, above)


def second_kernel(region_base, sub_odd, sub_even, odd_out, even_out):
    cs = Consts()
    sub_below, sub_above = arrivals(sub_even, sub_odd, "sub", 2)
    target = (cs.lane // 8) % 8
    whole = []
    for side in range(2):
        packed = region_base[16 * side : 16 * side + 8, :]
        info = region_base[16 * side + 8 : 16 * side + 16, :].astype(jnp.int32)
        order = row(info, 0)
        added = jnp.zeros((8, 128), jnp.float32)
        for f, message in ((2, sub_below), (3, sub_above)):
            place = row(info, f + 1)
            at = jnp.maximum(place, 0) % 8
            total = jnp.zeros((8, 128), jnp.float32)
            for i in range(8):
                got = lane_gather(message[0], 32 * (i % 2) + 8 * (i // 2) + at)
                got = jnp.where(i <= order, got, 0.0)
                total = total - got if side == 0 and i % 2 == 1 else total + got
            total = jnp.where(place >= 0, total, 0.0)
            if f == 2:
                total = jnp.where(target % 2 == 0, total, -total)
            added = added + total
        inside = jnp.maximum(target, cs.k) <= order
        inside = jnp.logical_and(inside, cs.lane >= 64)
        added = added * (CORNER * (2 * target + 1).astype(jnp.float32))
        packed = packed + jnp.where(inside, added, 0.0)
        below, above = sub_below[1], sub_above[1]
        if side == 0:
            relay = jnp.where(cs.lane < 64, below, pltpu.roll(above, 64, 1))
        else:
            relay = jnp.where(cs.lane < 64, pltpu.roll(below, 64, 1), above)
        whole.append((packed, relay))
    even = even_index("region")
    for n in range(2):
        low, high = whole[0][n], whole[1][n]
        even_out[8 * n : 8 * n + 8, :] = pick(even, high, low)
        odd_out[8 * n : 8 * n + 8, :] = pick(even, low, high)


def third_kernel(
    fields_in, stored_in, tables, sub_odd, sub_even, region_odd, region_even,
    state_far, register_far, state_out, register_out, left,
):
    cs = Consts()
    order, source, index, wall = [tables[8 * n : 8 * n + 8, :] for n in range(4)]
    sub_side = arrivals(sub_even, sub_odd, "sub", 3)
    region_side = arrivals(region_even, region_odd, "region", 2)
    keep = kept(cs, order)
    step = jnp.stack([jnp.where(c, TIME_STEP, 0.0) for c in keep])
    fields = [fields_in[128 * q : 128 * q + 128, :].reshape(16, 8, 128) for q in range(4)]
    stored = [stored_in[128 * q : 128 * q + 128, :].reshape(16, 8, 128) for q in range(4)]

    def arrived(kind, seconds):
        waves = []
        for side in range(2):
            at = 64 * kind + row(index, side) % 8
            message = region_side[side][0]
            waves.append(jnp.stack([lane_gather(message, at + 8 * j) for j in range(8)]))
        for side in range(2):
            at = 64 * kind + 8 * cs.t + row(index, 2 + side) % 8
            message = seconds[side] if kind else sub_side[side][0]
            waves.append(jnp.stack([lane_gather(message, at + 32 * il) for il in range(2)]))
        return waves

    first = arrived(0, None)
    first = [jnp.where((row(source, f) == f + 1)[None], first[f], 0.0) for f in range(4)]
    rate_p = None
    for axis in range(2):
        low, high = first[2 * axis], first[2 * axis + 1]
        gain_p, gain_u = spread(axis, (low + high) * 0.25, (high - low) * 0.25, cs)
        fac = factors(axis, cs)
        part = times(fac, gain_p)
        rate_p = part if axis == 0 else rate_p + part
        change = step * times(fac, gain_u)
        stored[1 + axis] = stored[1 + axis] + change
        fields[1 + axis] = fields[1 + axis] + SECTION_B[0] * change
    change = step * rate_p
    stored[0] = stored[0] + change
    fields[0] = fields[0] + SECTION_B[0] * change

    target = (cs.lane // 32) % 2 + 2 * ((cs.lane // 8) % 4)
    seconds = []
    for side in range(2):
        packed, _, info = sub_side[side]
        info = info.astype(jnp.int32)
        their_order = row(info, 0)
        added = jnp.zeros((8, 128), jnp.float32)
        for f in range(2):
            place = row(info, f + 1)
            at = 64 * side + jnp.maximum(place, 0) % 8
            relay = region_side[f][1]
            total = mode_sum(relay, at, 8, 16, their_order, side == 1, cs)
            total = jnp.where(place >= 0, total, 0.0)
            if f == 0:
                total = jnp.where(target % 2 == 0, total, -total)
            added = added + total
        inside = jnp.maximum(target, cs.k) <= their_order
        inside = jnp.logical_and(inside, cs.lane >= 64)
        added = added * (CORNER * (2 * target + 1).astype(jnp.float32))
        seconds.append(packed + jnp.where(inside, added, 0.0))

    out, inn, nexts = traces(fields, cs)
    outside = outside_waves(out, source, index, wall, cs, arrived(1, seconds))
    rate = rates(out, inn, nexts, outside, cs)
    fields, stored = section_step(1, fields, stored, rate, step)
    back = cs.weights(-1)
    copies = []
    for n, (values, ref, far) in enumerate(
        ((stored, register_out, register_far), (fields, state_out, state_far))
    ):
        for q in range(4):
            store_field(ref, q, values[q] * back)
        copies.append(pltpu.make_async_copy(ref, far, left.at[n]))
        copies[n].start()
    for copy in copies:
        copy.wait()


def swap(x, axis_name, parity, count):
    pairs = []
    for i in range(parity, count - 1, 2):
        pairs += [(i, i + 1), (i + 1, i)]
    return lax.ppermute(x, axis_name, pairs)


def gather_pairs(x, axis_name, count):
    groups = [[i, i + 1] for i in range(0, count, 2)]
    return lax.all_gather(x, axis_name, axis_index_groups=groups, tiled=True)


def call(kernel, outs, scratch, ins=None, out_space=pltpu.VMEM, kinds=None):
    kinds = [jnp.float32] * len(outs) if kinds is None else kinds
    space = pl.BlockSpec(memory_space=out_space)
    specs = {} if ins is None else dict(in_specs=[pl.BlockSpec(memory_space=pltpu.HBM)] * ins)
    return pl.pallas_call(
        kernel,
        out_shape=[jax.ShapeDtypeStruct((n, 128), kind) for n, kind in zip(outs, kinds)],
        out_specs=[space] * len(outs),
        scratch_shapes=scratch,
        compiler_params=pltpu.CompilerParams(vmem_limit_bytes=32 * 1024 * 1024),
        **specs,
    )


def body(counts, state, register, orders, link_source, link_index, walls, send_region, send_sub):
    def tiles(x):
        return x.reshape(32, 4, 4, 128).transpose(0, 2, 1, 3).reshape(512, 128)

    def untiles(x):
        return x.reshape(32, 4, 4, 128).transpose(0, 2, 1, 3).reshape(32, 4, 512)

    def held(x):
        return pltpu.with_memory_space_constraint(x, pltpu.HBM)

    whole = [pltpu.VMEM((512, 128), jnp.float32)] * 2
    small = [pltpu.VMEM(shape, jnp.int32) for shape in ((1, 32), (6, 32), (6, 32), (6, 32), (2, 8), (2, 8))]
    floats, ints = jnp.float32, jnp.int32
    fields, stored, tables, region_base, odd, even = call(
        first_kernel,
        (512, 512, 32, 32, 24, 24),
        whole + small + [pltpu.VMEM((6, 8, 128), jnp.int32), pltpu.SemaphoreType.DMA((8,))],
        ins=8,
        kinds=(floats, floats, ints, floats, floats, floats),
    )(
        held(tiles(state)), held(tiles(register)), held(orders.reshape(1, 32)), held(link_source.T),
        held(link_index.T), held(walls.T), held(send_region[0]), held(send_sub[0]),
    )
    sub_odd = swap(odd, "sub", 1, counts["sub"])
    sub_even = gather_pairs(even, "sub", counts["sub"])
    odd, even = call(second_kernel, (16, 16), [])(region_base, sub_odd, sub_even)
    region_odd = swap(odd, "region", 1, counts["region"])
    region_even = gather_pairs(even, "region", counts["region"])
    state, register = call(
        third_kernel, (512, 512), whole + [pltpu.SemaphoreType.DMA((2,))], out_space=pltpu.HBM
    )(fields, stored, tables, sub_odd, sub_even, region_odd, region_even)
    return (untiles(state), untiles(register))


def solution(mesh):
    both = P(("region", "sub"))
    return jax.shard_map(
        functools.partial(body, dict(mesh.shape)),
        mesh=mesh,
        in_specs=(both,) * 8,
        out_specs=(both, both),
        check_vma=False,
    )
```
